256 devices in a mesh: band: 32 (over z_hi, y, core), grid: 8 (over z_lo, x).
Axes of the slice: x: 4, y: 4, z: 8 (z_hi: 4, z_lo: 2; z = z_hi * 2 + z_lo), core: 2. Of those that a mesh axis runs over, the one named last changes fastest.
Arguments:
- block_coeffs: float32 [256, 32768], P('band', 'grid'), may hold values from -6 to 6
- potential: float32 [96, 9216], P('grid'), may hold values from -4 to 4
- lower_edge: float32 [1], replicated, may hold values from 0.8 to 1.2
- upper_edge: float32 [1], replicated, may hold values from 4.5 to 5.5
- rotation: float32 [8, 6144, 8], P(None, 'band'), may hold values from -0.75 to 0.75
- owners: int32 [8], replicated, may hold values from 0 to 31
Outputs:
- filtered: float32 [256, 32768], P('band', 'grid')
- residents: float32 [6144, 32768], P('band', 'grid')
The draws below stay inside these ranges and needn't reach their ends.
All inputs are finite; a program needn't handle non-finite values.
Results may differ from the reference program's by a relative error of at most 0.000071.
Values sent between devices are 32-bit elements; how exact they have to be, the bound alone decides.
A program may use at most 64 MiB of HBM per device.

```python
import jax
import jax.numpy as jnp
from jax import lax

NG = 96
KEEP = 32
BLK = 8
STEPS = 8
BANDS = 256
RBANDS = 6144
NPW = 32768
PLANE = 9216
N_BAND = 32


def plant(drawn, rng, low, top_value):
    spot = [jax.random.randint(jax.random.fold_in(rng, axis), (), 0, length) for axis, length in enumerate(drawn.shape)]
    main_axis = drawn.shape.index(max(drawn.shape))
    next_to = spot[:main_axis] + [(spot[main_axis] + 1) % drawn.shape[main_axis]] + spot[main_axis + 1:]
    return drawn.at[tuple(spot)].set(low).at[tuple(next_to)].set(top_value)


def shard_levels(own_key, shape, split, smallest, top_value):
    level = 1.0
    for dim, blocks in split:
        draws = jax.random.uniform(jax.random.fold_in(jax.random.fold_in(own_key, 6), dim), (blocks,), jnp.float32, smallest / len(split), top_value / len(split))
        level = level * jnp.repeat(jnp.exp(draws), shape[dim] // blocks).reshape((-1,) + (1,) * (len(shape) - 1 - dim))
    return level


def bell_draw(key, dims, spread, limit, shards=(), kind=jnp.bfloat16):
    result = jax.random.normal(key, dims, jnp.float32) * spread
    if len(shards) > 0:
        result = shard_levels(key, dims, shards, -0.22, 0.18) * result
    return jnp.clip(result, min=-limit, max=limit).astype(kind)


def setup_inputs(seed: int = 0) -> dict:
    key_of = jax.random.split(jax.random.key(seed), 7)
    return {
        "block_coeffs": bell_draw(key_of[0], (BANDS, NPW), 1.0, 6.0, ((0, 32), (1, 8)), jnp.float32),
        "potential": bell_draw(key_of[1], (NG, PLANE), 1.0, 4.0, ((0, 8),), jnp.float32),
        "lower_edge": jnp.clip(jax.random.uniform(key_of[2], (1,), jnp.float32, 0.8, 1.2), 0.8, 1.2),
        "upper_edge": jnp.clip(jax.random.uniform(key_of[3], (1,), jnp.float32, 4.5, 5.5), 4.5, 5.5),
        "rotation": bell_draw(key_of[4], (STEPS, RBANDS, BLK), (BLK * STEPS) ** -0.5, 0.75, ((1, 32),), jnp.float32),
        "owners": plant(jax.random.randint(key_of[5], (STEPS,), 0, N_BAND), jax.random.fold_in(key_of[5], 1), 0, N_BAND - 1).astype(jnp.int32),
    }


edge_energy = 1.3

def kept_frequency(kept_count, grid_points):
    ordinal = jnp.arange(kept_count, dtype=jnp.int32)
    return jnp.where(ordinal < kept_count // 2, ordinal, ordinal + (grid_points - kept_count))

def hartley_table(kept_count, grid_points):
    points = jnp.arange(grid_points, dtype=jnp.int32)
    phase_turns = points[:, None] * kept_frequency(kept_count, grid_points)[None, :] % grid_points
    angles = phase_turns.astype(jnp.float32) * (2.0 * jnp.pi / grid_points)
    return (jnp.cos(angles) + jnp.sin(angles)) / jnp.sqrt(jnp.float32(grid_points))

def signed_square(kept_count):
    ordinal = jnp.arange(kept_count, dtype=jnp.int32)
    signed = jnp.where(ordinal < kept_count // 2, ordinal, ordinal - kept_count).astype(jnp.float32)
    return signed * signed / jnp.float32((kept_count // 2) ** 2)

def kinetic_cube(kept_count):
    square = signed_square(kept_count)
    return edge_energy * (square[:, None, None] + square[None, :, None] + square[None, None, :])

def synthesize(coeffs, hartley):
    coef_cube = coeffs.reshape(coeffs.shape[0], KEEP, KEEP, KEEP)
    along_x = jnp.einsum('bqkz,nk->bqnz', coef_cube, hartley, precision=lax.Precision.HIGHEST)
    along_y = jnp.einsum('bqnz,yq->bnyz', along_x, hartley, precision=lax.Precision.HIGHEST)
    return jnp.einsum('bnyz,wz->bnyw', along_y, hartley, precision=lax.Precision.HIGHEST)

def analyse(real_field, hartley):
    along_z = jnp.einsum('bnyw,wz->bnyz', real_field, hartley, precision=lax.Precision.HIGHEST)
    along_y = jnp.einsum('bnyz,yq->bqnz', along_z, hartley, precision=lax.Precision.HIGHEST)
    along_x = jnp.einsum('bqnz,nk->bqkz', along_y, hartley, precision=lax.Precision.HIGHEST)
    return along_x.reshape(real_field.shape[0], NPW)

def reference(block_coeffs, potential, lower_edge, upper_edge, rotation, owners):
    hartley = hartley_table(KEEP, NG)
    kinetic = kinetic_cube(KEEP).reshape(1, NPW)
    potential_cube = potential.reshape(NG, NG, NG)
    center = (lower_edge[0] + upper_edge[0]) * 0.5
    half_width = (upper_edge[0] - lower_edge[0]) * 0.5

    def hamiltonian(coeffs):
        return kinetic * coeffs + analyse(potential_cube[None] * synthesize(coeffs, hartley), hartley)

    def filter_group(coeffs):
        first_term = (hamiltonian(coeffs) - center * coeffs) / half_width
        return 2.0 * (hamiltonian(first_term) - center * first_term) / half_width - coeffs
    grouped = lax.map(filter_group, block_coeffs.reshape(N_BAND, BLK, NPW))
    filtered = grouped.reshape(BANDS, NPW)
    stacked = grouped[owners]
    residents = jnp.einsum('sri,sin->rn', rotation, stacked, precision=lax.Precision.HIGHEST)
    return (filtered, residents)
```

```python
import functools

import jax
import jax.numpy as jnp
import ml_dtypes
import numpy as np
from jax import lax
from jax.experimental import pallas as pl
from jax.experimental.pallas import tpu as pltpu
from jax.sharding import PartitionSpec as P

NG = 96
KEEP = 32
SHARDS = 8
BANDS = 8
GROUPS = 32
STEPS = 8
edge_energy = 1.3

F32 = jnp.float32
BF16 = jnp.bfloat16
MESH = pl.DeviceIdType.MESH


def split_table(table):
    hi = table.astype(ml_dtypes.bfloat16)
    lo = (table - hi.astype(np.float64)).astype(ml_dtypes.bfloat16)
    return hi, lo


def hartley_table():
    ordinal = np.arange(KEEP)
    frequency = np.where(ordinal < KEEP // 2, ordinal, ordinal + NG - KEEP)
    angle = (np.arange(NG)[:, None] * frequency[None, :] % NG) * (2.0 * np.pi / NG)
    return (np.cos(angle) + np.sin(angle)) / np.sqrt(float(NG))


def tables():
    hi, lo = split_table(hartley_table())
    zero = np.zeros((), ml_dtypes.bfloat16)
    order = np.array([4 * (r % 24) + r // 24 for r in range(NG)])
    y_syn = np.concatenate([hi, lo, hi, lo], 1)[order]
    block_hi = np.kron(np.eye(4), hi.T.astype(np.float32)).astype(hi.dtype)
    block_lo = np.kron(np.eye(4), lo.T.astype(np.float32)).astype(hi.dtype)
    z_syn = np.concatenate([np.concatenate([block_hi, block_lo], 1)] * 2, 0)
    stacked = np.concatenate([hi, lo, hi, lo], 1)
    x_syn = np.full((SHARDS, 2, 12, 2, 128), zero)
    for half in range(2):
        x_syn[:, half, :, half] = stacked.reshape(SHARDS, 12, 128)
    x_syn = x_syn.reshape(192, 256)
    parts = []
    for t in (hi, lo):
        part = np.full((2, KEEP, SHARDS, 2, 12), zero)
        for half in range(2):
            part[half, :, :, half, :] = t.T.reshape(KEEP, SHARDS, 12)
        parts.append(part.reshape(64, 192))
    x_ana = np.concatenate(parts, 0)
    z_ana = np.concatenate([np.concatenate([block_hi.T, block_lo.T], 1)] * 2, 0)
    y_ana = np.concatenate([np.concatenate([t[order].T] * 2, 1) for t in (hi, lo)], 0)
    signed = np.where(np.arange(KEEP) < KEEP // 2, np.arange(KEEP), np.arange(KEEP) - KEEP)
    square = (signed * signed / float((KEEP // 2) ** 2)).astype(np.float32)
    kinetic = np.float32(edge_energy) * (
        square[:, None, None] + square[None, :, None] + square[None, None, :]
    )
    return y_syn, z_syn, x_syn, x_ana, z_ana, y_ana, kinetic.reshape(KEEP, KEEP * KEEP)


def split(x):
    hi = x.astype(BF16)
    return hi, (x - hi.astype(F32)).astype(BF16)


def dot(a, b):
    return jnp.dot(a, b, preferred_element_type=F32)


def swap_groups(parts):
    lane = lax.broadcasted_iota(jnp.int32, parts[0].shape, 1)
    low = lane < 64
    even = lane % 64 < 32
    half = [None] * 4
    for j in range(2):
        half[j] = jnp.where(low, parts[j], pltpu.roll(parts[j + 2], 64, 1))
        half[j + 2] = jnp.where(low, pltpu.roll(parts[j], 64, 1), parts[j + 2])
    out = []
    for a, b in ((half[0], half[1]), (half[2], half[3])):
        out.append(jnp.where(even, a, pltpu.roll(b, 32, 1)))
        out.append(jnp.where(even, pltpu.roll(a, 96, 1), b))
    return out


def expand_rows(c, tabs, scratch):
    y_syn, z_syn = tabs[:2]
    d1, d2h, d2l, _ = scratch
    ch, cl = split(c)
    along_y = dot(y_syn[...], jnp.concatenate([ch, ch, cl, cl], 0))
    for k8 in range(8):
        cols = slice(128 * k8, 128 * k8 + 128)
        parts = swap_groups([along_y[24 * j : 24 * j + 24, cols] for j in range(4)])
        for m in range(4):
            d1[pl.ds((4 * k8 + m) * 24, 24), :] = parts[m]
    for i in range(6):
        rows = jnp.concatenate([d1[pl.ds(4 * i + j, 32, stride=24), :] for j in range(4)], 0)
        rh, rl = split(rows)
        wide = dot(jnp.concatenate([rh, rl], 1), z_syn[...])
        dh, dl = split(wide[:, :384] + wide[:, 384:])
        d2h[pl.ds(128 * i, 128), :] = dh
        d2l[pl.ds(128 * i, 128), :] = dl


def cross_planes(column, v, tabs, scratch):
    _, _, x_syn, x_ana, _, _ = tabs
    _, d2h, d2l, bz = scratch

    def plane_step(i, carry):
        q = column * 6 + i
        r0 = pl.multiple_of(q * 32, 32)
        r1 = pl.multiple_of(q * 32 + 384, 32)
        h0, l0 = d2h[pl.ds(r0, 32), :], d2l[pl.ds(r0, 32), :]
        h1, l1 = d2h[pl.ds(r1, 32), :], d2l[pl.ds(r1, 32), :]
        field = dot(x_syn[...], jnp.concatenate([h0, h0, l0, l0, h1, h1, l1, l1], 0))
        at = pl.multiple_of(i * 384, 128)
        wh, wl = split(field * v[column, :, :, pl.ds(at, 384)].reshape(192, 384))
        first = dot(x_ana[...], wh)
        back = first[:64] + first[64:] + dot(x_ana[pl.ds(0, 64), :], wl)
        bh, bl = split(back)
        bz[pl.ds(r0, 32), pl.ds(0, 384)] = bh[:32]
        bz[pl.ds(r0, 32), pl.ds(384, 384)] = bl[:32]
        bz[pl.ds(r1, 32), pl.ds(0, 384)] = bh[32:]
        bz[pl.ds(r1, 32), pl.ds(384, 384)] = bl[32:]
        return carry

    lax.fori_loop(0, 6, plane_step, 0, unroll=2)


def contract_rows(tabs, scratch):
    z_ana, y_ana = tabs[4:]
    d1, _, _, bz = scratch
    for i in range(3):
        wide = dot(bz[pl.ds(256 * i, 256), :], z_ana[...])
        d1[pl.ds(256 * i, 256), :] = wide[:, :128] + wide[:, 128:]
    columns = []
    for k8 in range(8):
        parts = [d1[pl.ds(4 * k8 + m, 24, stride=32), :] for m in range(4)]
        columns.append(jnp.concatenate(swap_groups(parts), 0))
    gh, gl = split(jnp.concatenate(columns, 1))
    back = dot(y_ana[...], jnp.concatenate([gh, gl], 0))
    return back[:32] + back[32:]


H_SCRATCH = [
    pltpu.VMEM((768, 128), F32),
    pltpu.VMEM((768, 384), BF16),
    pltpu.VMEM((768, 384), BF16),
    pltpu.VMEM((768, 768), BF16),
]


def filter_kernel(x_ref, v_ref, lower, upper, owners, *refs):
    tabs, kinetic = refs[:6], refs[6]
    filtered, arrived = refs[7:9]
    scratch = refs[9:13]
    (v, pack, coeffs, spread, landed, chunk, gathered, blocks,
     a_send, a_recv, v_send, v_recv, b_send, b_recv, c_send, c_recv, out_sem) = refs[13:]
    band = lax.axis_index("band")
    grid = lax.axis_index("grid")
    z_hi, y, core = band // 8, (band // 2) % 4, band % 2
    z_lo, x = grid // 4, grid % 4
    sibling = (z_hi * 8 + y * 2 + 1 - core, grid)

    def z_step(step):
        z = (z_hi * 2 + z_lo + step) % 8
        return ((z // 2) * 8 + band % 8, (1 - z_lo) * 4 + x)

    def x_step(step):
        return (band, z_lo * 4 + (x + step) % 4)

    def remote(src, dst, send, recv, to):
        return pltpu.make_async_remote_copy(
            src_ref=src, dst_ref=dst, send_sem=send, recv_sem=recv, device_id=to, device_id_type=MESH
        )

    barrier = pltpu.get_barrier_semaphore()

    def greet(to):
        pl.semaphore_signal(barrier, inc=1, device_id=to, device_id_type=MESH)

    @pl.loop(1, SHARDS)
    def _(d):
        greet((band, (grid + d) % SHARDS))

    @pl.loop(1, GROUPS)
    def _(d):
        greet(((band + d) % GROUPS, grid))

    greet(z_step(1))
    greet(z_step(7))

    for r in range(32):
        pack[pl.ds(r, 8, stride=32), :] = x_ref[:, 128 * r : 128 * r + 128]
    for half in range(2):
        for c in range(2):
            at = 4608 * half + 2304 * c
            v[c, grid, pl.ds(12 * half, 12), :] = v_ref[:, at : at + 2304]
    pl.semaphore_wait(barrier, SHARDS - 1 + GROUPS - 1 + 2)

    def exchange(src, dst, first_sem):
        def copy(d, to, block, slot):
            return remote(
                src.at[pl.ds(pl.multiple_of(block * 32, 32), 32), :],
                dst.at[pl.ds(pl.multiple_of(slot * 32, 32), 32), :],
                a_send.at[first_sem + d], a_recv.at[first_sem + d], (band, to),
            )

        def start():
            for d in range(1, SHARDS):
                to = (grid + d) % SHARDS
                copy(d, to, to, grid).start()
            own = pl.ds(pl.multiple_of(grid * 32, 32), 32)
            dst[own, :] = src[own, :]

        def wait():
            for d in range(1, SHARDS):
                came = (grid + SHARDS - d) % SHARDS
                copy(d, came, came, came).wait_recv()

        def wait_sent():
            for d in range(1, SHARDS):
                to = (grid + d) % SHARDS
                copy(d, to, to, grid).wait_send()

        return start, wait, wait_sent

    near = [z_lo * 4 + (x + s) % 4 for s in (0, 3, 1, 2)]
    far = [(1 - z_lo) * 4 + (x + s) % 4 for s in (0, 3, 1, 2)]

    def v_copy(sem, shard, to, piece=None):
        lanes = pl.ds(0, 2304) if piece is None else pl.ds(1152 * piece, 1152)
        ref = v.at[core, shard, :, lanes]
        return remote(ref, ref, v_send.at[sem], v_recv.at[sem], to)

    sent = []

    def v_go(sem, shard, to, piece=None):
        copy = v_copy(sem, shard, to, piece)
        copy.start()
        sent.append(copy)

    def v_come(sem, shard, piece=None):
        v_copy(sem, shard, sibling, piece).wait_recv()

    in_start, in_wait, in_sent = exchange(pack, coeffs, 0)
    in_start()
    v_go(0, near[0], x_step(1))
    v_go(1, near[0], x_step(3))
    for piece, step in ((0, 1), (1, 7)):
        v_go(4 + piece, near[0], z_step(step), piece)
    in_wait()
    c = jnp.concatenate([coeffs[pl.ds(k8, 32, stride=8), :] for k8 in range(8)], 1)
    center = (lower[0] + upper[0]) * 0.5
    inverse = 1.0 / ((upper[0] - lower[0]) * 0.5)
    expand_rows(c, tabs, scratch)

    v_come(0, near[1])
    v_go(2, near[1], x_step(1), 0)
    v_come(1, near[2])
    v_go(3, near[2], x_step(3), 1)
    for s in (1, 2):
        for piece, step in ((0, 1), (1, 7)):
            v_go(4 + 2 * s + piece, near[s], z_step(step), piece)
        v_go(11 + s, near[s], sibling)
    for piece, step in ((0, 1), (1, 7)):
        v_come(2 + piece, near[3], piece)
        v_go(10 + piece, near[3], z_step(step), piece)
        v_go(14 + piece, near[3], sibling, piece)
    for s in range(4):
        for piece in range(2):
            v_come(4 + 2 * s + piece, far[s], piece)
            v_go(16 + 2 * s + piece, far[s], sibling, piece)
    cross_planes(core, v, tabs, scratch)

    def v_twin(sem, shard, piece=None):
        lanes = pl.ds(0, 2304) if piece is None else pl.ds(1152 * piece, 1152)
        ref = v.at[1 - core, shard, :, lanes]
        remote(ref, ref, v_send.at[sem], v_recv.at[sem], sibling).wait_recv()

    v_twin(12, near[1])
    v_twin(13, near[2])
    for piece in range(2):
        v_twin(14 + piece, near[3], piece)
        for s in range(4):
            v_twin(16 + 2 * s + piece, far[s], piece)
    cross_planes(1 - core, v, tabs, scratch)
    shift = kinetic[...] - center
    first = (shift * c + contract_rows(tabs, scratch)) * inverse
    expand_rows(first, tabs, scratch)
    cross_planes(0, v, tabs, scratch)
    cross_planes(1, v, tabs, scratch)
    second = shift * first + contract_rows(tabs, scratch)
    out = (2.0 * inverse) * second - c
    for k8 in range(8):
        spread[pl.ds(k8, 32, stride=8), :] = out[:, 128 * k8 : 128 * k8 + 128]
    out_start, out_wait, out_sent = exchange(spread, landed, SHARDS)
    out_start()
    for copy in sent:
        copy.wait_send()
    in_sent()
    out_wait()
    for r in range(32):
        rows = landed[pl.ds(r, 8, stride=32), :]
        filtered[:, 128 * r : 128 * r + 128] = rows
        chunk[r] = rows

    def b_copy(d, to, block, slot):
        return remote(chunk.at[block], blocks.at[slot], b_send.at[d], b_recv.at[d], (to, grid))

    @pl.loop(1, GROUPS)
    def _(d):
        to = (band + d) % GROUPS
        b_copy(d, to, to, band).start()

    blocks[band] = chunk[band]

    @pl.loop(1, GROUPS)
    def _(d):
        came = (band + GROUPS - d) % GROUPS
        b_copy(d, came, came, came).wait_recv()

    for s in range(STEPS):
        gathered[band, pl.ds(8 * s, 8), :] = blocks[owners[s]]

    def c_copy(sem, index, to):
        ref = gathered.at[index]
        return remote(ref, ref, c_send.at[sem], c_recv.at[sem], (to, grid))

    def index_of(dz, dy, other):
        k = 1 - core if other else core
        return ((z_hi + 4 - dz) % 4) * 8 + ((y + 4 - dy) % 4) * 2 + k

    away = sibling[0]
    for dz in range(1, 4):
        c_copy(dz, band, ((z_hi + dz) % 4) * 8 + band % 8).start()
    for dz in range(4):
        mine = index_of(dz, 0, False)
        if dz:
            c_copy(dz, mine, away).wait_recv()
        for dy in range(1, 4):
            c_copy(4 + 3 * dz + dy - 1, mine, z_hi * 8 + ((y + dy) % 4) * 2 + core).start()
        c_copy(16 + 4 * dz, mine, away).start()
    for dz in range(4):
        for dy in range(1, 4):
            mine = index_of(dz, dy, False)
            c_copy(4 + 3 * dz + dy - 1, mine, away).wait_recv()
            c_copy(16 + 4 * dz + dy, mine, away).start()
    for dz in range(4):
        for dy in range(4):
            c_copy(16 + 4 * dz + dy, index_of(dz, dy, True), away).wait_recv()
    write = pltpu.make_async_copy(gathered, arrived, out_sem)
    write.start()

    @pl.loop(1, GROUPS)
    def _(d):
        to = (band + d) % GROUPS
        b_copy(d, to, to, band).wait_send()

    @pl.loop(1, 32)
    def _(d):
        c_copy(d, band, away).wait_send()

    out_sent()
    write.wait()


VMEM = pl.BlockSpec(memory_space=pltpu.VMEM)
SMEM = pl.BlockSpec(memory_space=pltpu.SMEM)
FILTER = pl.pallas_call(
    filter_kernel,
    out_shape=(
        jax.ShapeDtypeStruct((8, 4096), F32),
        jax.ShapeDtypeStruct((GROUPS, 64, 128), F32),
    ),
    in_specs=[VMEM, VMEM, SMEM, SMEM, SMEM] + [VMEM] * 7,
    out_specs=(VMEM, pl.BlockSpec(memory_space=pl.ANY)),
    scratch_shapes=H_SCRATCH + [
        pltpu.VMEM((2, SHARDS, 24, 2304), F32),
        pltpu.VMEM((256, 128), F32),
        pltpu.VMEM((256, 128), F32),
        pltpu.VMEM((256, 128), F32),
        pltpu.VMEM((256, 128), F32),
        pltpu.VMEM((32, 8, 128), F32),
        pltpu.VMEM((GROUPS, 64, 128), F32),
        pltpu.VMEM((GROUPS, 8, 128), F32),
        pltpu.SemaphoreType.DMA((16,)),
        pltpu.SemaphoreType.DMA((16,)),
        pltpu.SemaphoreType.DMA((24,)),
        pltpu.SemaphoreType.DMA((24,)),
        pltpu.SemaphoreType.DMA((32,)),
        pltpu.SemaphoreType.DMA((32,)),
        pltpu.SemaphoreType.DMA((32,)),
        pltpu.SemaphoreType.DMA((32,)),
        pltpu.SemaphoreType.DMA,
    ],
    compiler_params=pltpu.CompilerParams(
        collective_id=0, has_side_effects=True, vmem_limit_bytes=40 << 20
    ),
    name="filter",
)


def rotate_kernel(rotation, arrived, filtered, filtered_out, residents):
    rh, rl = split(rotation[...])
    left = jnp.concatenate([rh, rl, rh, rl], 1)
    for j in range(4):
        ah, al = split(arrived[j])
        residents[:, 128 * j : 128 * j + 128] = dot(left, jnp.concatenate([ah, ah, al, al], 0))
    filtered_out[...] = filtered[...]


ROTATE = pl.pallas_call(
    rotate_kernel,
    grid=(8,),
    out_shape=(
        jax.ShapeDtypeStruct((8, 4096), F32),
        jax.ShapeDtypeStruct((192, 4096), F32),
    ),
    in_specs=[
        pl.BlockSpec((192, 64), lambda i: (0, 0)),
        pl.BlockSpec((4, 64, 128), lambda i: (i, 0, 0)),
        pl.BlockSpec((8, 512), lambda i: (0, i)),
    ],
    out_specs=(
        pl.BlockSpec((8, 512), lambda i: (0, i)),
        pl.BlockSpec((192, 512), lambda i: (0, i)),
    ),
    name="rotate",
)


def body(block_coeffs, potential, lower_edge, upper_edge, rotation, owners):
    consts = [jnp.asarray(t) for t in tables()]
    filtered, arrived = FILTER(
        block_coeffs, potential, lower_edge, upper_edge, owners, *consts
    )
    coefficients = rotation.transpose(1, 0, 2).reshape(192, 64)
    return tuple(ROTATE(coefficients, arrived, filtered))


def solution(mesh):
    return jax.shard_map(
        body,
        mesh=mesh,
        in_specs=(P("band", "grid"), P("grid", None), P(), P(), P(None, "band", None), P()),
        out_specs=(P("band", "grid"), P("band", "grid")),
        check_vma=False,
    )
```

```python
import functools

import jax
import jax.numpy as jnp
import ml_dtypes
import numpy as np
from jax import lax
from jax.experimental import pallas as pl
from jax.experimental.pallas import tpu as pltpu
from jax.sharding import PartitionSpec as P

NG = 96
KEEP = 32
NS = 64
SHARDS = 8
BANDS = 8
GROUPS = 32
STEPS = 8
edge_energy = 1.3

F32 = jnp.float32
BF16 = jnp.bfloat16
MESH = pl.DeviceIdType.MESH
VMEM_LIMIT = 58 << 20


def split_table(table):
    hi = table.astype(ml_dtypes.bfloat16)
    lo = (table - hi.astype(np.float64)).astype(ml_dtypes.bfloat16)
    return hi, lo


def hartley_table():
    ordinal = np.arange(KEEP)
    frequency = np.where(ordinal < KEEP // 2, ordinal, ordinal + NG - KEEP)
    angle = (np.arange(NG)[:, None] * frequency[None, :] % NG) * (2.0 * np.pi / NG)
    return (np.cos(angle) + np.sin(angle)) / np.sqrt(float(NG))


def fine_points():
    return np.arange(NG) * (2.0 * np.pi / NG)


def short_points():
    return (np.arange(NS) + 0.5) * (2.0 * np.pi / NS)


def short_table():
    ordinal = np.arange(KEEP)
    signed = np.where(ordinal < KEEP // 2, ordinal, ordinal - KEEP)
    angle = short_points()[:, None] * signed[None, :]
    return (np.cos(angle) + np.sin(angle)) / np.sqrt(float(NG))


def resample_table():
    gap = short_points()[:, None] - fine_points()[None, :]
    table = 1.0 + 2.0 * sum(np.cos(f * gap) for f in range(1, KEEP))
    table = table + np.sin(KEEP * short_points())[:, None] * np.sin(KEEP * fine_points())[None, :]
    return table / NS


def four_blocks(table):
    return np.kron(np.eye(4), table.astype(np.float32)).astype(table.dtype)


def tables():
    hi, lo = split_table(hartley_table())
    short_hi, short_lo = split_table(short_table())
    fit_hi, fit_lo = split_table(resample_table())
    zero = np.zeros((), ml_dtypes.bfloat16)
    order = np.array([4 * (r % 16) + r // 16 for r in range(NS)])
    y_syn = np.concatenate([short_hi, short_lo, short_hi, short_lo], 1)[order]
    z_syn = np.concatenate([four_blocks(short_hi.T), four_blocks(short_lo.T)], 1)
    stacked = np.concatenate([hi, lo, hi, lo], 1)
    x_syn = np.full((SHARDS, 2, 12, 2, 128), zero)
    for half in range(2):
        x_syn[:, half, :, half] = stacked.reshape(SHARDS, 12, 128)
    x_syn = x_syn.reshape(192, 256)
    parts = []
    for t in (hi, lo):
        part = np.full((2, KEEP, SHARDS, 2, 12), zero)
        for half in range(2):
            part[half, :, :, half, :] = t.T.reshape(KEEP, SHARDS, 12)
        parts.append(part.reshape(64, 192))
    x_ana = np.concatenate(parts, 0)
    z_ana = np.concatenate([four_blocks(short_hi), four_blocks(short_lo)], 1)
    y_ana = np.concatenate([np.concatenate([t[order].T] * 2, 1) for t in (short_hi, short_lo)], 0)
    z_fit = np.concatenate([four_blocks(fit_hi.T), four_blocks(fit_lo.T)], 1)
    rows = np.array([2 * (r % 32) + r // 32 for r in range(NS)])
    columns = np.array([4 * (r % 24) + r // 24 for r in range(NG)])
    y_fit = np.concatenate([t[rows][:, columns] for t in (fit_hi, fit_lo, fit_hi, fit_lo)], 1)
    return y_syn, z_syn, x_syn, x_ana, z_ana, y_ana, z_fit, y_fit


def kinetic_plane():
    def square(k):
        signed = jnp.where(k < KEEP // 2, k, k - KEEP)
        return (signed * signed).astype(F32) * (1.0 / (KEEP // 2) ** 2)

    ky = lax.broadcasted_iota(jnp.int32, (KEEP, KEEP * KEEP), 0)
    lane = lax.broadcasted_iota(jnp.int32, (KEEP, KEEP * KEEP), 1)
    return edge_energy * (square(ky) + square(lane // KEEP) + square(lane % KEEP))


def split(x):
    hi = x.astype(BF16)
    return hi, (x - hi.astype(F32)).astype(BF16)


def dot(a, b):
    return jnp.dot(a, b, preferred_element_type=F32)


def swap_groups(parts):
    lane = lax.broadcasted_iota(jnp.int32, parts[0].shape, 1)
    low = lane < 64
    even = lane % 64 < 32
    half = [None] * 4
    for j in range(2):
        half[j] = jnp.where(low, parts[j], pltpu.roll(parts[j + 2], 64, 1))
        half[j + 2] = jnp.where(low, pltpu.roll(parts[j], 64, 1), parts[j + 2])
    out = []
    for a, b in ((half[0], half[1]), (half[2], half[3])):
        out.append(jnp.where(even, a, pltpu.roll(b, 32, 1)))
        out.append(jnp.where(even, pltpu.roll(a, 96, 1), b))
    return out


def twofold(a, table, width):
    ah, al = split(a)
    wide = dot(ah, table[...])
    return wide[:, :width] + wide[:, width:] + dot(al, table[:, :width])


def fit_potential(v_ref, tabs, planes, own):
    z_fit, y_fit = tabs[6:]
    lane = lax.broadcasted_iota(jnp.int32, (32, 128), 1)
    low = lane < 64
    blank = jnp.zeros((4, 384), F32)
    for i in range(4):
        blocks = []
        for c in range(6 * i, 6 * i + 6):
            blocks += [v_ref[:, 384 * c : 384 * c + 384], blank]
        rows = jnp.concatenate(blocks, 0)
        fit = twofold(rows, z_fit, 256)
        for tile in range(2):
            planes[tile, pl.ds(96 * i, 96), :] = fit[:, 128 * tile : 128 * tile + 128]
    columns = []
    for n in range(0, 12, 2):
        parts = []
        for j in range(4):
            a = planes[j // 2, pl.ds(n, 24, stride=16), :]
            b = planes[j // 2, pl.ds(n + 1, 24, stride=16), :]
            if j % 2 == 0:
                parts.append(jnp.where(low[:24], a, pltpu.roll(b, 64, 1)))
            else:
                parts.append(jnp.where(low[:24], pltpu.roll(a, 64, 1), b))
        columns.append(jnp.concatenate(parts, 0))
    hi, lo = split(jnp.concatenate(columns, 1))
    fit = dot(y_fit[...], jnp.concatenate([hi, hi, lo, lo], 0))
    for n in range(0, 12, 2):
        even, odd = fit[:32, 64 * n : 64 * n + 128], fit[32:, 64 * n : 64 * n + 128]
        first = jnp.where(low, even, pltpu.roll(odd, 64, 1))
        second = jnp.where(low, pltpu.roll(even, 64, 1), odd)
        for p, plane in ((n, first), (n + 1, second)):
            for half in range(2):
                for column in range(2):
                    t = 16 * half + 8 * column
                    own[pl.ds(192 * column + 12 * half + p, 8, stride=24), :] = plane[t : t + 8]


def expand_rows(c, tabs, scratch):
    y_syn, z_syn = tabs[:2]
    d1, d2h, d2l, _ = scratch
    ch, cl = split(c)
    along_y = dot(y_syn[...], jnp.concatenate([ch, ch, cl, cl], 0))
    for k8 in range(8):
        cols = slice(128 * k8, 128 * k8 + 128)
        parts = swap_groups([along_y[16 * j : 16 * j + 16, cols] for j in range(4)])
        for m in range(4):
            d1[pl.ds((4 * k8 + m) * 16, 16), :] = parts[m]
    for i in range(2):
        rows = jnp.concatenate([d1[pl.ds(8 * i + j, 32, stride=16), :] for j in range(8)], 0)
        dh, dl = split(twofold(rows, z_syn, 256))
        d2h[pl.ds(256 * i, 256), :] = dh
        d2l[pl.ds(256 * i, 256), :] = dl


def cross_planes(column, v, tabs, scratch):
    _, _, x_syn, x_ana = tabs[:4]
    _, d2h, d2l, bz = scratch

    def plane_step(i, carry):
        q = column * 4 + i
        r0 = pl.multiple_of(q * 32, 32)
        r1 = pl.multiple_of(q * 32 + 256, 32)
        h0, l0 = d2h[pl.ds(r0, 32), :], d2l[pl.ds(r0, 32), :]
        h1, l1 = d2h[pl.ds(r1, 32), :], d2l[pl.ds(r1, 32), :]
        field = dot(x_syn[...], jnp.concatenate([h0, h0, l0, l0, h1, h1, l1, l1], 0))
        tiles = [
            v[column, :, pl.ds(pl.multiple_of(48 * i + 24 * j, 8), 24), :].reshape(192, 128)
            for j in range(2)
        ]
        wh, wl = split(field * jnp.concatenate(tiles, 1))
        first = dot(x_ana[...], wh)
        back = first[:64] + first[64:] + dot(x_ana[pl.ds(0, 64), :], wl)
        bz[pl.ds(r0, 32), :] = back[:32]
        bz[pl.ds(r1, 32), :] = back[32:]
        return carry

    lax.fori_loop(0, 4, plane_step, 0, unroll=True)


def contract_rows(tabs, scratch):
    z_ana, y_ana = tabs[4:6]
    d1, _, _, bz = scratch
    for i in range(2):
        d1[pl.ds(256 * i, 256), :] = twofold(bz[pl.ds(256 * i, 256), :], z_ana, 128)
    columns = []
    for k8 in range(8):
        parts = [d1[pl.ds(4 * k8 + m, 16, stride=32), :] for m in range(4)]
        columns.append(jnp.concatenate(swap_groups(parts), 0))
    gh, gl = split(jnp.concatenate(columns, 1))
    back = dot(y_ana[...], jnp.concatenate([gh, gl], 0))
    return back[:32] + back[32:]


H_SCRATCH = [
    pltpu.VMEM((512, 128), F32),
    pltpu.VMEM((512, 256), BF16),
    pltpu.VMEM((512, 256), BF16),
    pltpu.VMEM((512, 256), F32),
]


def filter_kernel(x_hbm, v_hbm, rotation_hbm, lower, upper, owners, *refs):
    tables_hbm = refs[:8]
    filtered, residents = refs[8:10]
    x_ref, v_ref, rotation_ref = refs[10:13]
    tabs = refs[13:21]
    scratch = refs[21:25]
    (v, planes, own, pack, coeffs, spread, landed, chunk, gathered, blocks, left, rotated, local_sem,
     a_send, a_recv, v_send, v_recv, b_send, b_recv, c_send, c_recv, out_sem) = refs[25:]
    band = lax.axis_index("band")
    grid = lax.axis_index("grid")
    z_hi, y, core = band // 8, (band // 2) % 4, band % 2
    z_lo, x = grid // 4, grid % 4
    sibling = (z_hi * 8 + y * 2 + 1 - core, grid)

    def z_step(step):
        z = (z_hi * 2 + z_lo + step) % 8
        return ((z // 2) * 8 + band % 8, (1 - z_lo) * 4 + x)

    def x_step(step):
        return (band, z_lo * 4 + (x + step) % 4)

    def y_step(step):
        return (z_hi * 8 + ((y + step) % 4) * 2 + core, grid)

    def remote(src, dst, send, recv, to):
        return pltpu.make_async_remote_copy(
            src_ref=src, dst_ref=dst, send_sem=send, recv_sem=recv, device_id=to, device_id_type=MESH
        )

    sources = (x_hbm, v_hbm, tables_hbm[6], tables_hbm[7], rotation_hbm) + tuple(tables_hbm[:6])
    targets = (x_ref, v_ref, tabs[6], tabs[7], rotation_ref) + tuple(tabs[:6])
    fetches = [
        pltpu.make_async_copy(src, dst, local_sem.at[i])
        for i, (src, dst) in enumerate(zip(sources, targets))
    ]
    for fetch in fetches:
        fetch.start()

    barrier = pltpu.get_barrier_semaphore()

    def greet(to):
        pl.semaphore_signal(barrier, inc=1, device_id=to, device_id_type=MESH)

    @pl.loop(1, SHARDS)
    def _(d):
        greet((band, (grid + d) % SHARDS))

    @pl.loop(1, GROUPS)
    def _(d):
        greet(((band + d) % GROUPS, grid))

    greet(z_step(1))
    greet(z_step(7))

    fetches[0].wait()
    for r in range(32):
        pack[pl.ds(r, 8, stride=32), :] = x_ref[:, 128 * r : 128 * r + 128]
    pl.semaphore_wait(barrier, SHARDS - 1 + GROUPS - 1 + 2)

    def exchange(src, dst, first_sem):
        def copy(d, to, block, slot):
            return remote(
                src.at[pl.ds(pl.multiple_of(block * 32, 32), 32), :],
                dst.at[pl.ds(pl.multiple_of(slot * 32, 32), 32), :],
                a_send.at[first_sem + d], a_recv.at[first_sem + d], (band, to),
            )

        def start():
            for d in range(1, SHARDS):
                to = (grid + d) % SHARDS
                copy(d, to, to, grid).start()
            own = pl.ds(pl.multiple_of(grid * 32, 32), 32)
            dst[own, :] = src[own, :]

        def wait():
            for d in range(1, SHARDS):
                came = (grid + SHARDS - d) % SHARDS
                copy(d, came, came, came).wait_recv()

        def wait_sent():
            for d in range(1, SHARDS):
                to = (grid + d) % SHARDS
                copy(d, to, to, grid).wait_send()

        return start, wait, wait_sent

    near = [z_lo * 4 + (x + s) % 4 for s in (0, 3, 1, 2)]
    far = [(1 - z_lo) * 4 + (x + s) % 4 for s in (0, 3, 1, 2)]

    def v_copy(sem, shard, to, part=None, column=core):
        rows = pl.ds(0, 192) if part is None else pl.ds(96 * part, 96)
        ref = v.at[column, shard, rows, :]
        return remote(ref, ref, v_send.at[sem], v_recv.at[sem], to)

    sent = []

    def v_go(*where):
        copy = v_copy(*where)
        copy.start()
        sent.append(copy)

    def along_z(s):
        for part, step in ((0, 1), (1, 7)):
            v_go(3 + 2 * s + part, near[s], z_step(step), part)

    def from_x(s):
        v_copy(s - 1, near[s], sibling).wait_recv()
        along_z(s)
        v_go(10 + s, near[s], sibling)

    def from_z(s):
        for part in range(2):
            v_copy(3 + 2 * s + part, far[s], sibling, part).wait_recv()
        v_go(14 + s, far[s], sibling)

    in_start, in_wait, in_sent = exchange(pack, coeffs, 0)
    in_start()
    for fetch in fetches[1:4]:
        fetch.wait()
    fit_potential(v_ref, tabs, planes, own)
    for column in range(2):
        v[column, grid] = own[192 * column : 192 * column + 192]
    for s, step in ((1, 1), (2, 3), (3, 2)):
        v_go(s - 1, near[0], x_step(step))
    along_z(0)
    for fetch in fetches[4:]:
        fetch.wait()
    rh, rl = split(rotation_ref[...].T)
    left[...] = jnp.concatenate([rh, rl, rh, rl], 1)
    center = (lower[0] + upper[0]) * 0.5
    inverse = 1.0 / ((upper[0] - lower[0]) * 0.5)
    in_wait()
    c = jnp.concatenate([coeffs[pl.ds(k8, 32, stride=8), :] for k8 in range(8)], 1)
    expand_rows(c, tabs, scratch)
    from_z(0)
    for s in range(1, 4):
        from_x(s)
    for s in range(1, 4):
        from_z(s)
    cross_planes(core, v, tabs, scratch)
    for s in range(1, 4):
        v_copy(10 + s, near[s], sibling, None, 1 - core).wait_recv()
    for s in range(4):
        v_copy(14 + s, far[s], sibling, None, 1 - core).wait_recv()
    cross_planes(1 - core, v, tabs, scratch)
    shift = kinetic_plane() - center
    first = (shift * c + contract_rows(tabs, scratch)) * inverse
    expand_rows(first, tabs, scratch)
    cross_planes(0, v, tabs, scratch)
    cross_planes(1, v, tabs, scratch)
    second = shift * first + contract_rows(tabs, scratch)
    out = (2.0 * inverse) * second - c
    for k8 in range(8):
        spread[pl.ds(k8, 32, stride=8), :] = out[:, 128 * k8 : 128 * k8 + 128]
    out_start, out_wait, out_sent = exchange(spread, landed, SHARDS)
    out_start()
    for copy in sent:
        copy.wait_send()
    in_sent()
    out_wait()
    for r in range(32):
        rows = landed[pl.ds(r, 8, stride=32), :]
        x_ref[:, 128 * r : 128 * r + 128] = rows
        chunk[r] = rows

    def b_copy(d, to, block, slot):
        return remote(chunk.at[block], blocks.at[slot], b_send.at[d], b_recv.at[d], (to, grid))

    @pl.loop(1, GROUPS)
    def _(d):
        to = (band + d) % GROUPS
        b_copy(d, to, to, band).start()

    write = pltpu.make_async_copy(x_ref, filtered, local_sem.at[0])
    write.start()
    blocks[band] = chunk[band]

    @pl.loop(1, GROUPS)
    def _(d):
        came = (band + GROUPS - d) % GROUPS
        b_copy(d, came, came, came).wait_recv()

    for s in range(STEPS):
        gathered[band, pl.ds(8 * s, 8), :] = blocks[owners[s]]

    def c_copy(sem, index, to):
        ref = gathered.at[index]
        return remote(ref, ref, c_send.at[sem], c_recv.at[sem], (to, grid))

    def index_of(dz, dy, other):
        k = 1 - core if other else core
        return ((z_hi + 4 - dz) % 4) * 8 + ((y + 4 - dy) % 4) * 2 + k

    away = sibling[0]
    for dz in range(1, 4):
        c_copy(dz, band, ((z_hi + dz) % 4) * 8 + band % 8).start()
    for dz in range(4):
        mine = index_of(dz, 0, False)
        if dz:
            c_copy(dz, mine, away).wait_recv()
        for dy in range(1, 4):
            c_copy(4 + 3 * dz + dy - 1, mine, z_hi * 8 + ((y + dy) % 4) * 2 + core).start()
        c_copy(16 + 4 * dz, mine, away).start()
    for dz in range(4):
        for dy in range(1, 4):
            mine = index_of(dz, dy, False)
            c_copy(4 + 3 * dz + dy - 1, mine, away).wait_recv()
            c_copy(16 + 4 * dz + dy, mine, away).start()

    writes = []
    for dz in range(4):
        for dy in range(4):
            c_copy(16 + 4 * dz + dy, index_of(dz, dy, True), away).wait_recv()
            pair = ((z_hi + 4 - dz) % 4) * 4 + (y + 4 - dy) % 4
            ah, al = split(jnp.concatenate([gathered[2 * pair], gathered[2 * pair + 1]], 1))
            at = pl.ds(pl.multiple_of(pair * 256, 256), 256)
            rotated[:, at] = dot(left[...], jnp.concatenate([ah, ah, al, al], 0))
            writes.append(pltpu.make_async_copy(rotated.at[:, at], residents.at[:, at], out_sem.at[4 * dz + dy]))
            writes[-1].start()

    @pl.loop(1, GROUPS)
    def _(d):
        to = (band + d) % GROUPS
        b_copy(d, to, to, band).wait_send()

    @pl.loop(1, 32)
    def _(d):
        c_copy(d, band, away).wait_send()

    out_sent()
    write.wait()
    for copy in writes:
        copy.wait()


SMEM = pl.BlockSpec(memory_space=pltpu.SMEM)
ANY = pl.BlockSpec(memory_space=pl.ANY)
FILTER = pl.pallas_call(
    filter_kernel,
    out_shape=(
        jax.ShapeDtypeStruct((8, 4096), F32),
        jax.ShapeDtypeStruct((192, 4096), F32),
    ),
    in_specs=[ANY] * 3 + [SMEM] * 3 + [ANY] * 8,
    out_specs=(ANY, ANY),
    scratch_shapes=[
        pltpu.VMEM((8, 4096), F32),
        pltpu.VMEM((12, 9216), F32),
        pltpu.VMEM((64, 192), F32),
        pltpu.VMEM((64, 128), BF16),
        pltpu.VMEM((128, 512), BF16),
        pltpu.VMEM((192, 256), BF16),
        pltpu.VMEM((128, 192), BF16),
        pltpu.VMEM((256, 256), BF16),
        pltpu.VMEM((64, 128), BF16),
        pltpu.VMEM((384, 512), BF16),
        pltpu.VMEM((64, 384), BF16),
    ] + H_SCRATCH + [
        pltpu.VMEM((2, SHARDS, 192, 128), F32),
        pltpu.VMEM((2, 384, 128), F32),
        pltpu.VMEM((384, 128), F32),
        pltpu.VMEM((256, 128), F32),
        pltpu.VMEM((256, 128), F32),
        pltpu.VMEM((256, 128), F32),
        pltpu.VMEM((256, 128), F32),
        pltpu.VMEM((32, 8, 128), F32),
        pltpu.VMEM((GROUPS, 64, 128), F32),
        pltpu.VMEM((GROUPS, 8, 128), F32),
        pltpu.VMEM((192, 256), BF16),
        pltpu.VMEM((192, 4096), F32),
        pltpu.SemaphoreType.DMA((11,)),
        pltpu.SemaphoreType.DMA((16,)),
        pltpu.SemaphoreType.DMA((16,)),
        pltpu.SemaphoreType.DMA((18,)),
        pltpu.SemaphoreType.DMA((18,)),
        pltpu.SemaphoreType.DMA((32,)),
        pltpu.SemaphoreType.DMA((32,)),
        pltpu.SemaphoreType.DMA((32,)),
        pltpu.SemaphoreType.DMA((32,)),
        pltpu.SemaphoreType.DMA((16,)),
    ],
    compiler_params=pltpu.CompilerParams(
        collective_id=0, has_side_effects=True, vmem_limit_bytes=VMEM_LIMIT
    ),
    name="filter",
)


def body(block_coeffs, potential, lower_edge, upper_edge, rotation, owners):
    consts = [jnp.asarray(t) for t in tables()]
    coefficients = rotation.transpose(0, 2, 1).reshape(64, 192)
    return tuple(
        FILTER(block_coeffs, potential, coefficients, lower_edge, upper_edge, owners, *consts)
    )


def solution(mesh):
    return jax.shard_map(
        body,
        mesh=mesh,
        in_specs=(P("band", "grid"), P("grid", None), P(), P(), P(None, "band", None), P()),
        out_specs=(P("band", "grid"), P("band", "grid")),
        check_vma=False,
    )
```

```python
import functools

import jax
import jax.numpy as jnp
import ml_dtypes
import numpy as np
from jax import lax
from jax.experimental import pallas as pl
from jax.experimental.pallas import tpu as pltpu
from jax.sharding import PartitionSpec as P

NG = 96
KEEP = 32
NS = 64
SHARDS = 8
BANDS = 8
GROUPS = 32
CHIPS = 16
STEPS = 8
edge_energy = 1.3

F32 = jnp.float32
BF16 = jnp.bfloat16
MESH = pl.DeviceIdType.MESH
VMEM_LIMIT = 58 << 20


def split_table(table):
    hi = table.astype(ml_dtypes.bfloat16)
    lo = (table - hi.astype(np.float64)).astype(ml_dtypes.bfloat16)
    return hi, lo


def hartley_table():
    ordinal = np.arange(KEEP)
    frequency = np.where(ordinal < KEEP // 2, ordinal, ordinal + NG - KEEP)
    angle = (np.arange(NG)[:, None] * frequency[None, :] % NG) * (2.0 * np.pi / NG)
    return (np.cos(angle) + np.sin(angle)) / np.sqrt(float(NG))


def fine_points():
    return np.arange(NG) * (2.0 * np.pi / NG)


def short_points():
    return (np.arange(NS) + 0.5) * (2.0 * np.pi / NS)


def short_table():
    ordinal = np.arange(KEEP)
    signed = np.where(ordinal < KEEP // 2, ordinal, ordinal - KEEP)
    angle = short_points()[:, None] * signed[None, :]
    return (np.cos(angle) + np.sin(angle)) / np.sqrt(float(NG))


def resample_table():
    gap = short_points()[:, None] - fine_points()[None, :]
    table = 1.0 + 2.0 * sum(np.cos(f * gap) for f in range(1, KEEP))
    table = table + np.sin(KEEP * short_points())[:, None] * np.sin(KEEP * fine_points())[None, :]
    return table / NS


def four_blocks(table):
    return np.kron(np.eye(4), table.astype(np.float32)).astype(table.dtype)


def tables():
    hi, lo = split_table(hartley_table())
    short_hi, short_lo = split_table(short_table())
    fit_hi, fit_lo = split_table(resample_table())
    zero = np.zeros((), ml_dtypes.bfloat16)
    order = np.array([4 * (r % 16) + r // 16 for r in range(NS)])
    y_syn = np.concatenate([short_hi, short_lo, short_hi, short_lo], 1)[order]
    z_syn = np.concatenate([four_blocks(short_hi.T), four_blocks(short_lo.T)], 1)
    stacked = np.concatenate([hi, lo, hi, lo], 1)
    x_syn = np.full((SHARDS, 2, 12, 2, 128), zero)
    for half in range(2):
        x_syn[:, half, :, half] = stacked.reshape(SHARDS, 12, 128)
    x_syn = x_syn.reshape(192, 256)
    parts = []
    for t in (hi, lo):
        part = np.full((2, KEEP, SHARDS, 2, 12), zero)
        for half in range(2):
            part[half, :, :, half, :] = t.T.reshape(KEEP, SHARDS, 12)
        parts.append(part.reshape(64, 192))
    x_ana = np.concatenate(parts, 0)
    z_ana = np.concatenate([four_blocks(short_hi), four_blocks(short_lo)], 1)
    y_ana = np.concatenate([np.concatenate([t[order].T] * 2, 1) for t in (short_hi, short_lo)], 0)
    z_fit = np.concatenate([four_blocks(fit_hi.T), four_blocks(fit_lo.T)], 1)
    rows = np.array([2 * (r % 32) + r // 32 for r in range(NS)])
    columns = np.array([4 * (r % 24) + r // 24 for r in range(NG)])
    y_fit = np.concatenate([t[rows][:, columns] for t in (fit_hi, fit_lo, fit_hi, fit_lo)], 1)
    return y_syn, z_syn, x_syn, x_ana, z_ana, y_ana, z_fit, y_fit


def kinetic_plane():
    def square(k):
        signed = jnp.where(k < KEEP // 2, k, k - KEEP)
        return (signed * signed).astype(F32) * (1.0 / (KEEP // 2) ** 2)

    ky = lax.broadcasted_iota(jnp.int32, (KEEP, KEEP * KEEP), 0)
    lane = lax.broadcasted_iota(jnp.int32, (KEEP, KEEP * KEEP), 1)
    return edge_energy * (square(ky) + square(lane // KEEP) + square(lane % KEEP))


def split(x):
    hi = x.astype(BF16)
    return hi, (x - hi.astype(F32)).astype(BF16)


def dot(a, b):
    return jnp.dot(a, b, preferred_element_type=F32)


def swap_groups(parts):
    lane = lax.broadcasted_iota(jnp.int32, parts[0].shape, 1)
    low = lane < 64
    even = lane % 64 < 32
    half = [None] * 4
    for j in range(2):
        half[j] = jnp.where(low, parts[j], pltpu.roll(parts[j + 2], 64, 1))
        half[j + 2] = jnp.where(low, pltpu.roll(parts[j], 64, 1), parts[j + 2])
    out = []
    for a, b in ((half[0], half[1]), (half[2], half[3])):
        out.append(jnp.where(even, a, pltpu.roll(b, 32, 1)))
        out.append(jnp.where(even, pltpu.roll(a, 96, 1), b))
    return out


def twofold(a, table, width):
    ah, al = split(a)
    wide = dot(ah, table[...])
    return wide[:, :width] + wide[:, width:] + dot(al, table[:, :width])


def fit_potential(v_ref, tabs, planes, own):
    z_fit, y_fit = tabs[6:]
    lane = lax.broadcasted_iota(jnp.int32, (32, 128), 1)
    low = lane < 64
    blank = jnp.zeros((4, 384), F32)
    for i in range(4):
        blocks = []
        for c in range(6 * i, 6 * i + 6):
            blocks += [v_ref[:, 384 * c : 384 * c + 384], blank]
        rows = jnp.concatenate(blocks, 0)
        fit = twofold(rows, z_fit, 256)
        for tile in range(2):
            planes[tile, pl.ds(96 * i, 96), :] = fit[:, 128 * tile : 128 * tile + 128]
    columns = []
    for n in range(0, 12, 2):
        parts = []
        for j in range(4):
            a = planes[j // 2, pl.ds(n, 24, stride=16), :]
            b = planes[j // 2, pl.ds(n + 1, 24, stride=16), :]
            if j % 2 == 0:
                parts.append(jnp.where(low[:24], a, pltpu.roll(b, 64, 1)))
            else:
                parts.append(jnp.where(low[:24], pltpu.roll(a, 64, 1), b))
        columns.append(jnp.concatenate(parts, 0))
    hi, lo = split(jnp.concatenate(columns, 1))
    fit = dot(y_fit[...], jnp.concatenate([hi, hi, lo, lo], 0))
    for n in range(0, 12, 2):
        even, odd = fit[:32, 64 * n : 64 * n + 128], fit[32:, 64 * n : 64 * n + 128]
        first = jnp.where(low, even, pltpu.roll(odd, 64, 1))
        second = jnp.where(low, pltpu.roll(even, 64, 1), odd)
        for p, plane in ((n, first), (n + 1, second)):
            for half in range(2):
                for column in range(2):
                    t = 16 * half + 8 * column
                    own[pl.ds(192 * column + 12 * half + p, 8, stride=24), :] = plane[t : t + 8]


def expand_rows(c, tabs, scratch):
    y_syn, z_syn = tabs[:2]
    d1, d2h, d2l, _ = scratch
    ch, cl = split(c)
    along_y = dot(y_syn[...], jnp.concatenate([ch, ch, cl, cl], 0))
    for k8 in range(8):
        cols = slice(128 * k8, 128 * k8 + 128)
        parts = swap_groups([along_y[16 * j : 16 * j + 16, cols] for j in range(4)])
        for m in range(4):
            d1[pl.ds((4 * k8 + m) * 16, 16), :] = parts[m]
    for i in range(2):
        rows = jnp.concatenate([d1[pl.ds(8 * i + j, 32, stride=16), :] for j in range(8)], 0)
        dh, dl = split(twofold(rows, z_syn, 256))
        d2h[pl.ds(256 * i, 256), :] = dh
        d2l[pl.ds(256 * i, 256), :] = dl


def cross_planes(column, v, tabs, scratch):
    _, _, x_syn, x_ana = tabs[:4]
    _, d2h, d2l, bz = scratch

    def plane_step(i, carry):
        q = column * 4 + i
        r0 = pl.multiple_of(q * 32, 32)
        r1 = pl.multiple_of(q * 32 + 256, 32)
        h0, l0 = d2h[pl.ds(r0, 32), :], d2l[pl.ds(r0, 32), :]
        h1, l1 = d2h[pl.ds(r1, 32), :], d2l[pl.ds(r1, 32), :]
        field = dot(x_syn[...], jnp.concatenate([h0, h0, l0, l0, h1, h1, l1, l1], 0))
        tiles = [
            v[column, :, pl.ds(pl.multiple_of(48 * i + 24 * j, 8), 24), :].reshape(192, 128)
            for j in range(2)
        ]
        wh, wl = split(field * jnp.concatenate(tiles, 1))
        first = dot(x_ana[...], wh)
        back = first[:64] + first[64:] + dot(x_ana[pl.ds(0, 64), :], wl)
        bz[pl.ds(r0, 32), :] = back[:32]
        bz[pl.ds(r1, 32), :] = back[32:]
        return carry

    lax.fori_loop(0, 4, plane_step, 0, unroll=True)


def contract_rows(tabs, scratch):
    z_ana, y_ana = tabs[4:6]
    d1, _, _, bz = scratch
    for i in range(2):
        d1[pl.ds(256 * i, 256), :] = twofold(bz[pl.ds(256 * i, 256), :], z_ana, 128)
    columns = []
    for k8 in range(8):
        parts = [d1[pl.ds(4 * k8 + m, 16, stride=32), :] for m in range(4)]
        columns.append(jnp.concatenate(swap_groups(parts), 0))
    gh, gl = split(jnp.concatenate(columns, 1))
    back = dot(y_ana[...], jnp.concatenate([gh, gl], 0))
    return back[:32] + back[32:]


H_SCRATCH = [
    pltpu.VMEM((512, 128), F32),
    pltpu.VMEM((512, 256), BF16),
    pltpu.VMEM((512, 256), BF16),
    pltpu.VMEM((512, 256), F32),
]


def filter_kernel(x_hbm, v_hbm, lower, upper, owners, *refs):
    tables_hbm = refs[:8]
    filtered, arrived = refs[8:10]
    x_ref, v_ref = refs[10:12]
    tabs = refs[12:20]
    scratch = refs[20:24]
    (v, planes, own, pack, coeffs, spread, landed, chunk, pairs, gathered, blocks, local_sem,
     a_send, a_recv, v_send, v_recv, b_send, b_recv, c_send, c_recv) = refs[24:]
    band = lax.axis_index("band")
    grid = lax.axis_index("grid")
    z_hi, y, core, chip = band // 8, (band // 2) % 4, band % 2, band // 2
    z_lo, x = grid // 4, grid % 4
    sibling = (z_hi * 8 + y * 2 + 1 - core, grid)

    def z_step(step):
        z = (z_hi * 2 + z_lo + step) % 8
        return ((z // 2) * 8 + band % 8, (1 - z_lo) * 4 + x)

    def x_step(step):
        return (band, z_lo * 4 + (x + step) % 4)

    def y_step(step):
        return (z_hi * 8 + ((y + step) % 4) * 2 + core, grid)

    def remote(src, dst, send, recv, to):
        return pltpu.make_async_remote_copy(
            src_ref=src, dst_ref=dst, send_sem=send, recv_sem=recv, device_id=to, device_id_type=MESH
        )

    sources = (v_hbm, tables_hbm[6], tables_hbm[7], x_hbm) + tuple(tables_hbm[:6])
    targets = (v_ref, tabs[6], tabs[7], x_ref) + tuple(tabs[:6])
    fetches = [
        pltpu.make_async_copy(src, dst, local_sem.at[i])
        for i, (src, dst) in enumerate(zip(sources, targets))
    ]
    for fetch in fetches:
        fetch.start()

    barrier = pltpu.get_barrier_semaphore()

    def greet(to):
        pl.semaphore_signal(barrier, inc=1, device_id=to, device_id_type=MESH)

    @pl.loop(1, SHARDS)
    def _(d):
        greet((band, (grid + d) % SHARDS))

    @pl.loop(1, CHIPS)
    def _(d):
        greet((((chip + d) % CHIPS) * 2 + core, grid))

    greet(sibling)
    greet(z_step(1))
    greet(z_step(7))

    for fetch in fetches[:3]:
        fetch.wait()
    fit_potential(v_ref, tabs, planes, own)
    for column in range(2):
        v[column, grid] = own[192 * column : 192 * column + 192]
    pl.semaphore_wait(barrier, SHARDS - 1 + CHIPS - 1 + 3)

    def exchange(src, dst, sem):
        def copy(to, block, slot, rows=32):
            return remote(
                src.at[pl.ds(pl.multiple_of(block * 32, 32), rows), :],
                dst.at[pl.ds(pl.multiple_of(slot * 32, 32), rows), :],
                a_send.at[sem], a_recv.at[sem], (band, to),
            )

        def start():
            for dz, dx in ((1, 2), (1, 1), (1, 3), (0, 2), (1, 0), (0, 1), (0, 3)):
                to = (z_lo + dz) % 2 * 4 + (x + dx) % 4
                copy(to, to, grid).start()
            own = pl.ds(pl.multiple_of(grid * 32, 32), 32)
            dst[own, :] = src[own, :]

        def all_of_them():
            return copy((grid + 1) % SHARDS, 0, 0, 32 * (SHARDS - 1))

        return start, all_of_them().wait_recv, all_of_them().wait_send

    near = [z_lo * 4 + (x + s) % 4 for s in (0, 3, 1, 2)]
    far = [(1 - z_lo) * 4 + (x + s) % 4 for s in (0, 3, 1, 2)]

    def v_copy(sem, shard, to, part=None, column=core):
        rows = pl.ds(0, 192) if part is None else pl.ds(96 * part, 96)
        ref = v.at[column, shard, rows, :]
        return remote(ref, ref, v_send.at[sem], v_recv.at[sem], to)

    sent = []

    def v_go(*where):
        copy = v_copy(*where)
        copy.start()
        sent.append(copy)

    def along_z(s, part):
        v_go(6 + 2 * s + part, near[s], z_step(7 if part else 1), part)

    def from_x(sem, s, part):
        v_copy(sem, near[s], sibling, part).wait_recv()
        along_z(s, part)

    def from_z(s):
        for part in range(2):
            v_copy(6 + 2 * s + part, far[s], sibling, part).wait_recv()
        v_go(17 + s, far[s], sibling)

    v_go(0, near[0], x_step(1), 0)
    v_go(3, near[0], x_step(3), 1)
    v_go(1, near[0], x_step(1), 1)
    v_go(2, near[0], x_step(3), 0)
    along_z(0, 0)
    along_z(0, 1)
    fetches[3].wait()
    for r in range(32):
        pack[pl.ds(r, 8, stride=32), :] = x_ref[:, 128 * r : 128 * r + 128]
    in_start, in_wait, in_sent = exchange(pack, coeffs, 0)
    in_start()
    center = (lower[0] + upper[0]) * 0.5
    inverse = 1.0 / ((upper[0] - lower[0]) * 0.5)
    for fetch in fetches[4:]:
        fetch.wait()
    from_x(0, 1, 0)
    v_go(4, near[1], x_step(1), 0)
    from_x(3, 2, 1)
    v_go(5, near[2], x_step(3), 1)
    from_x(1, 1, 1)
    v_go(14, near[1], sibling)
    from_x(2, 2, 0)
    v_go(15, near[2], sibling)
    in_wait()
    c = jnp.concatenate([coeffs[pl.ds(k8, 32, stride=8), :] for k8 in range(8)], 1)
    expand_rows(c, tabs, scratch)
    from_z(0)
    from_x(4, 3, 0)
    from_x(5, 3, 1)
    v_go(16, near[3], sibling)
    for s in range(1, 4):
        from_z(s)
    cross_planes(core, v, tabs, scratch)
    for s in range(1, 4):
        v_copy(13 + s, near[s], sibling, None, 1 - core).wait_recv()
    for s in range(4):
        v_copy(17 + s, far[s], sibling, None, 1 - core).wait_recv()
    cross_planes(1 - core, v, tabs, scratch)
    shift = kinetic_plane() - center
    first = (shift * c + contract_rows(tabs, scratch)) * inverse
    expand_rows(first, tabs, scratch)
    cross_planes(0, v, tabs, scratch)
    cross_planes(1, v, tabs, scratch)
    second = shift * first + contract_rows(tabs, scratch)
    out = (2.0 * inverse) * second - c
    for k8 in range(8):
        spread[pl.ds(k8, 32, stride=8), :] = out[:, 128 * k8 : 128 * k8 + 128]
    out_start, out_wait, out_sent = exchange(spread, landed, 1)
    out_start()
    for copy in sent:
        copy.wait_send()
    in_sent()
    out_wait()
    for r in range(32):
        rows = landed[pl.ds(r, 8, stride=32), :]
        x_ref[:, 128 * r : 128 * r + 128] = rows
        chunk[r % 2, r // 2] = rows
    write = pltpu.make_async_copy(x_ref, filtered, local_sem.at[0])
    write.start()

    swap = remote(chunk.at[1 - core], pairs.at[:, core], b_send.at[0], b_recv.at[0], sibling)
    swap.start()
    pairs[:, core] = chunk[core]
    remote(chunk.at[core], pairs.at[:, 1 - core], b_send.at[0], b_recv.at[0], sibling).wait_recv()

    for dz, dy in sorted(
        ((dz, dy) for dz in range(4) for dy in range(4) if dz + dy),
        key=lambda d: -2 * min(d[0], 4 - d[0]) - min(d[1], 4 - d[1]),
    ):
        to = (z_hi + dz) % 4 * 4 + (y + dy) % 4
        remote(pairs.at[to], blocks.at[chip], b_send.at[1], b_recv.at[1], (to * 2 + core, grid)).start()

    blocks[chip] = pairs[chip]
    all_chips = remote(
        pairs.at[pl.ds(0, CHIPS - 1)], blocks.at[pl.ds(0, CHIPS - 1)], b_send.at[1], b_recv.at[1], sibling
    )
    all_chips.wait_recv()
    for s in range(STEPS):
        gathered[band, pl.ds(8 * s, 8), :] = blocks[owners[s] // 2, owners[s] % 2]

    def c_copy(sem, index, to):
        ref = gathered.at[index]
        return remote(ref, ref, c_send, c_recv.at[sem], (to, grid))

    def index_of(dz, dy):
        return ((z_hi + 4 - dz) % 4) * 8 + ((y + 4 - dy) % 4) * 2 + core

    def deliver(index):
        pltpu.make_async_copy(gathered.at[index], arrived.at[index], local_sem.at[1]).start()
        remote(gathered.at[index], arrived.at[index], c_send, c_recv.at[0], sibling).start()

    def along_z_hi(dz):
        c_copy(dz, band, ((z_hi + dz) % 4) * 8 + band % 8).start()

    def along_y(dz):
        mine = index_of(dz, 0)
        for dy in (1, 3, 2):
            c_copy(4 + 3 * dz + dy - 1, mine, z_hi * 8 + ((y + dy) % 4) * 2 + core).start()
        deliver(mine)

    def from_y(dz):
        for dy in (1, 3, 2):
            mine = index_of(dz, dy)
            c_copy(4 + 3 * dz + dy - 1, mine, sibling[0]).wait_recv()
            deliver(mine)

    along_z_hi(1)
    along_z_hi(3)
    along_y(0)
    along_z_hi(2)
    for dz in (1, 3):
        c_copy(dz, index_of(dz, 0), sibling[0]).wait_recv()
        along_y(dz)
    from_y(0)
    c_copy(2, index_of(2, 0), sibling[0]).wait_recv()
    along_y(2)
    for dz in (1, 3, 2):
        from_y(dz)
    swap.wait_send()
    all_chips.wait_send()
    out_sent()
    write.wait()
    half = pl.ds(0, CHIPS)
    pltpu.make_async_copy(gathered.at[half], arrived.at[half], local_sem.at[1]).wait()
    remote(gathered.at[half], arrived.at[half], c_send, c_recv.at[0], sibling).wait_recv()
    every = pl.ds(0, GROUPS - 1)
    remote(gathered.at[every], arrived.at[every], c_send, c_recv.at[0], sibling).wait_send()


SMEM = pl.BlockSpec(memory_space=pltpu.SMEM)
ANY = pl.BlockSpec(memory_space=pl.ANY)
FILTER = pl.pallas_call(
    filter_kernel,
    out_shape=(
        jax.ShapeDtypeStruct((8, 4096), F32),
        jax.ShapeDtypeStruct((GROUPS, 64, 128), F32),
    ),
    in_specs=[ANY] * 2 + [SMEM] * 3 + [ANY] * 8,
    out_specs=(ANY, ANY),
    scratch_shapes=[
        pltpu.VMEM((8, 4096), F32),
        pltpu.VMEM((12, 9216), F32),
        pltpu.VMEM((64, 128), BF16),
        pltpu.VMEM((128, 512), BF16),
        pltpu.VMEM((192, 256), BF16),
        pltpu.VMEM((128, 192), BF16),
        pltpu.VMEM((256, 256), BF16),
        pltpu.VMEM((64, 128), BF16),
        pltpu.VMEM((384, 512), BF16),
        pltpu.VMEM((64, 384), BF16),
    ] + H_SCRATCH + [
        pltpu.VMEM((2, SHARDS, 192, 128), F32),
        pltpu.VMEM((2, 384, 128), F32),
        pltpu.VMEM((384, 128), F32),
        pltpu.VMEM((256, 128), F32),
        pltpu.VMEM((256, 128), F32),
        pltpu.VMEM((256, 128), F32),
        pltpu.VMEM((256, 128), F32),
        pltpu.VMEM((2, CHIPS, 8, 128), F32),
        pltpu.VMEM((CHIPS, 2, 8, 128), F32),
        pltpu.VMEM((GROUPS, 64, 128), F32),
        pltpu.VMEM((CHIPS, 2, 8, 128), F32),
        pltpu.SemaphoreType.DMA((10,)),
        pltpu.SemaphoreType.DMA((2,)),
        pltpu.SemaphoreType.DMA((2,)),
        pltpu.SemaphoreType.DMA((21,)),
        pltpu.SemaphoreType.DMA((21,)),
        pltpu.SemaphoreType.DMA((2,)),
        pltpu.SemaphoreType.DMA((2,)),
        pltpu.SemaphoreType.DMA,
        pltpu.SemaphoreType.DMA((16,)),
    ],
    compiler_params=pltpu.CompilerParams(
        collective_id=0, has_side_effects=True, vmem_limit_bytes=VMEM_LIMIT
    ),
    name="filter",
)


def rotate_kernel(rotation_hbm, arrived, filtered, filtered_out, residents, rotation, rows, block, rotated, in_sem, out_sem):
    get_rotation = pltpu.make_async_copy(rotation_hbm, rotation, in_sem.at[0])
    get_filtered = pltpu.make_async_copy(filtered, block, in_sem.at[1])
    get_rows = [
        pltpu.make_async_copy(arrived.at[pl.ds(4 * i, 4)], rows.at[pl.ds(4 * i, 4)], in_sem.at[2 + i])
        for i in range(8)
    ]
    get_rotation.start()
    for get in get_rows:
        get.start()
    get_filtered.start()
    get_rotation.wait()
    rh, rl = split(rotation[...].T)
    left = jnp.concatenate([rh, rl, rh, rl], 1)
    writes = [pltpu.make_async_copy(block, filtered_out, out_sem.at[8])]
    for i in range(8):
        get_rows[i].wait()
        ah, al = split(jnp.concatenate([rows[4 * i + j] for j in range(4)], 1))
        at = pl.ds(512 * i, 512)
        rotated[:, at] = dot(left, jnp.concatenate([ah, ah, al, al], 0))
        writes.append(pltpu.make_async_copy(rotated.at[:, at], residents.at[:, at], out_sem.at[i]))
        writes[-1].start()
        if i == 0:
            get_filtered.wait()
            writes[0].start()
    for write in writes:
        write.wait()


ROTATE = pl.pallas_call(
    rotate_kernel,
    out_shape=(
        jax.ShapeDtypeStruct((8, 4096), F32),
        jax.ShapeDtypeStruct((192, 4096), F32),
    ),
    in_specs=[ANY] * 3,
    out_specs=(ANY, ANY),
    scratch_shapes=[
        pltpu.VMEM((64, 192), F32),
        pltpu.VMEM((GROUPS, 64, 128), F32),
        pltpu.VMEM((8, 4096), F32),
        pltpu.VMEM((192, 4096), F32),
        pltpu.SemaphoreType.DMA((10,)),
        pltpu.SemaphoreType.DMA((9,)),
    ],
    compiler_params=pltpu.CompilerParams(vmem_limit_bytes=VMEM_LIMIT),
    name="rotate",
)


def body(block_coeffs, potential, lower_edge, upper_edge, rotation, owners):
    consts = [jnp.asarray(t) for t in tables()]
    filtered, arrived = FILTER(block_coeffs, potential, lower_edge, upper_edge, owners, *consts)
    coefficients = rotation.transpose(0, 2, 1).reshape(64, 192)
    return tuple(ROTATE(coefficients, arrived, filtered))


def solution(mesh):
    return jax.shard_map(
        body,
        mesh=mesh,
        in_specs=(P("band", "grid"), P("grid", None), P(), P(), P(None, "band", None), P()),
        out_specs=(P("band", "grid"), P("band", "grid")),
        check_vma=False,
    )
```

```python
import functools

import jax
import jax.numpy as jnp
import ml_dtypes
import numpy as np
from jax import lax
from jax.experimental import pallas as pl
from jax.experimental.pallas import tpu as pltpu
from jax.sharding import PartitionSpec as P

NG = 96
KEEP = 32
NS = 64
SHARDS = 8
BANDS = 8
GROUPS = 32
CHIPS = 16
STEPS = 8
edge_energy = 1.3

F32 = jnp.float32
BF16 = jnp.bfloat16
MESH = pl.DeviceIdType.MESH
VMEM_LIMIT = 58 << 20


def split_table(table):
    hi = table.astype(ml_dtypes.bfloat16)
    lo = (table - hi.astype(np.float64)).astype(ml_dtypes.bfloat16)
    return hi, lo


def hartley_table():
    ordinal = np.arange(KEEP)
    frequency = np.where(ordinal < KEEP // 2, ordinal, ordinal + NG - KEEP)
    angle = (np.arange(NG)[:, None] * frequency[None, :] % NG) * (2.0 * np.pi / NG)
    return (np.cos(angle) + np.sin(angle)) / np.sqrt(float(NG))


def fine_points():
    return np.arange(NG) * (2.0 * np.pi / NG)


def short_points():
    return (np.arange(NS) + 0.5) * (2.0 * np.pi / NS)


def short_table():
    ordinal = np.arange(KEEP)
    signed = np.where(ordinal < KEEP // 2, ordinal, ordinal - KEEP)
    angle = short_points()[:, None] * signed[None, :]
    return (np.cos(angle) + np.sin(angle)) / np.sqrt(float(NG))


def resample_table():
    gap = short_points()[:, None] - fine_points()[None, :]
    table = 1.0 + 2.0 * sum(np.cos(f * gap) for f in range(1, KEEP))
    table = table + np.sin(KEEP * short_points())[:, None] * np.sin(KEEP * fine_points())[None, :]
    return table / NS


def four_blocks(table):
    return np.kron(np.eye(4), table.astype(np.float32)).astype(table.dtype)


def tables():
    hi, lo = split_table(hartley_table())
    short_hi, short_lo = split_table(short_table())
    fit_hi, fit_lo = split_table(resample_table())
    zero = np.zeros((), ml_dtypes.bfloat16)
    order = np.array([4 * (r % 16) + r // 16 for r in range(NS)])
    y_syn = np.concatenate([short_hi, short_lo, short_hi, short_lo], 1)[order]
    z_syn = np.concatenate([four_blocks(short_hi.T), four_blocks(short_lo.T)], 1)
    stacked = np.concatenate([hi, lo, hi, lo], 1)
    x_syn = np.full((SHARDS, 2, 12, 2, 128), zero)
    for half in range(2):
        x_syn[:, half, :, half] = stacked.reshape(SHARDS, 12, 128)
    x_syn = x_syn.reshape(192, 256)
    parts = []
    for t in (hi, lo):
        part = np.full((2, KEEP, SHARDS, 2, 12), zero)
        for half in range(2):
            part[half, :, :, half, :] = t.T.reshape(KEEP, SHARDS, 12)
        parts.append(part.reshape(64, 192))
    x_ana = np.concatenate(parts, 0)
    z_ana = np.concatenate([four_blocks(short_hi), four_blocks(short_lo)], 1)
    y_ana = np.concatenate([np.concatenate([t[order].T] * 2, 1) for t in (short_hi, short_lo)], 0)
    z_fit = np.concatenate([four_blocks(fit_hi.T), four_blocks(fit_lo.T)], 1)
    rows = np.array([2 * (r % 32) + r // 32 for r in range(NS)])
    columns = np.array([4 * (r % 24) + r // 24 for r in range(NG)])
    y_fit = np.concatenate([t[rows][:, columns] for t in (fit_hi, fit_lo, fit_hi, fit_lo)], 1)
    return y_syn, z_syn, x_syn, x_ana, z_ana, y_ana, z_fit, y_fit


def kinetic_plane():
    def square(k):
        signed = jnp.where(k < KEEP // 2, k, k - KEEP)
        return (signed * signed).astype(F32) * (1.0 / (KEEP // 2) ** 2)

    ky = lax.broadcasted_iota(jnp.int32, (KEEP, KEEP * KEEP), 0)
    lane = lax.broadcasted_iota(jnp.int32, (KEEP, KEEP * KEEP), 1)
    return edge_energy * (square(ky) + square(lane // KEEP) + square(lane % KEEP))


def split(x):
    hi = x.astype(BF16)
    return hi, (x - hi.astype(F32)).astype(BF16)


def dot(a, b):
    return jnp.dot(a, b, preferred_element_type=F32)


def swap_groups(parts):
    lane = lax.broadcasted_iota(jnp.int32, parts[0].shape, 1)
    low = lane < 64
    even = lane % 64 < 32
    half = [None] * 4
    for j in range(2):
        half[j] = jnp.where(low, parts[j], pltpu.roll(parts[j + 2], 64, 1))
        half[j + 2] = jnp.where(low, pltpu.roll(parts[j], 64, 1), parts[j + 2])
    out = []
    for a, b in ((half[0], half[1]), (half[2], half[3])):
        out.append(jnp.where(even, a, pltpu.roll(b, 32, 1)))
        out.append(jnp.where(even, pltpu.roll(a, 96, 1), b))
    return out


def twofold(a, table, width):
    ah, al = split(a)
    wide = dot(ah, table[...])
    return wide[:, :width] + wide[:, width:] + dot(al, table[:, :width])


def fit_potential(v_ref, tabs, planes, own):
    z_fit, y_fit = tabs[6:]
    lane = lax.broadcasted_iota(jnp.int32, (32, 128), 1)
    low = lane < 64
    blank = jnp.zeros((4, 384), F32)
    blocks = []
    for c in range(24):
        blocks += [v_ref[:, 384 * c : 384 * c + 384], blank]
    fit = twofold(jnp.concatenate(blocks, 0), z_fit, 256)
    for tile in range(2):
        planes[tile] = fit[:, 128 * tile : 128 * tile + 128]
    columns = []
    for n in range(0, 12, 2):
        parts = []
        for j in range(4):
            a = planes[j // 2, pl.ds(n, 24, stride=16), :]
            b = planes[j // 2, pl.ds(n + 1, 24, stride=16), :]
            if j % 2 == 0:
                parts.append(jnp.where(low[:24], a, pltpu.roll(b, 64, 1)))
            else:
                parts.append(jnp.where(low[:24], pltpu.roll(a, 64, 1), b))
        columns.append(jnp.concatenate(parts, 0))
    hi, lo = split(jnp.concatenate(columns, 1))
    fit = dot(y_fit[...], jnp.concatenate([hi, hi, lo, lo], 0))
    for n in range(0, 12, 2):
        even, odd = fit[:32, 64 * n : 64 * n + 128], fit[32:, 64 * n : 64 * n + 128]
        first = jnp.where(low, even, pltpu.roll(odd, 64, 1))
        second = jnp.where(low, pltpu.roll(even, 64, 1), odd)
        for p, plane in ((n, first), (n + 1, second)):
            for half in range(2):
                for column in range(2):
                    t = 16 * half + 8 * column
                    own[pl.ds(192 * column + 12 * half + p, 8, stride=24), :] = plane[t : t + 8]


def expand_rows(c, tabs, scratch):
    y_syn, z_syn = tabs[:2]
    d1, d2h, d2l, _ = scratch
    ch, cl = split(c)
    along_y = dot(y_syn[...], jnp.concatenate([ch, ch, cl, cl], 0))
    for k8 in range(8):
        cols = slice(128 * k8, 128 * k8 + 128)
        parts = swap_groups([along_y[16 * j : 16 * j + 16, cols] for j in range(4)])
        for m in range(4):
            d1[pl.ds((4 * k8 + m) * 16, 16), :] = parts[m]
    for i in range(2):
        rows = jnp.concatenate([d1[pl.ds(8 * i + j, 32, stride=16), :] for j in range(8)], 0)
        dh, dl = split(twofold(rows, z_syn, 256))
        d2h[pl.ds(256 * i, 256), :] = dh
        d2l[pl.ds(256 * i, 256), :] = dl


def cross_planes(column, v, tabs, scratch):
    _, _, x_syn, x_ana = tabs[:4]
    _, d2h, d2l, bz = scratch

    def plane_step(i, carry):
        q = column * 4 + i
        r0 = pl.multiple_of(q * 32, 32)
        r1 = pl.multiple_of(q * 32 + 256, 32)
        h0, l0 = d2h[pl.ds(r0, 32), :], d2l[pl.ds(r0, 32), :]
        h1, l1 = d2h[pl.ds(r1, 32), :], d2l[pl.ds(r1, 32), :]
        field = dot(x_syn[...], jnp.concatenate([h0, h0, l0, l0, h1, h1, l1, l1], 0))
        tiles = [
            v[column, :, pl.ds(pl.multiple_of(48 * i + 24 * j, 8), 24), :].reshape(192, 128)
            for j in range(2)
        ]
        wh, wl = split(field * jnp.concatenate(tiles, 1))
        first = dot(x_ana[...], wh)
        back = first[:64] + first[64:] + dot(x_ana[pl.ds(0, 64), :], wl)
        bz[pl.ds(r0, 32), :] = back[:32]
        bz[pl.ds(r1, 32), :] = back[32:]
        return carry

    lax.fori_loop(0, 4, plane_step, 0, unroll=True)


def contract_rows(tabs, scratch):
    z_ana, y_ana = tabs[4:6]
    d1, _, _, bz = scratch
    for i in range(2):
        d1[pl.ds(256 * i, 256), :] = twofold(bz[pl.ds(256 * i, 256), :], z_ana, 128)
    columns = []
    for k8 in range(8):
        parts = [d1[pl.ds(4 * k8 + m, 16, stride=32), :] for m in range(4)]
        columns.append(jnp.concatenate(swap_groups(parts), 0))
    gh, gl = split(jnp.concatenate(columns, 1))
    back = dot(y_ana[...], jnp.concatenate([gh, gl], 0))
    return back[:32] + back[32:]


H_SCRATCH = [
    pltpu.VMEM((512, 128), F32),
    pltpu.VMEM((512, 256), BF16),
    pltpu.VMEM((512, 256), BF16),
    pltpu.VMEM((512, 256), F32),
]


def filter_kernel(x_hbm, v_hbm, rotation_hbm, lower, upper, owners, *refs):
    tables_hbm = refs[:8]
    filtered, residents = refs[8:10]
    x_ref, v_ref = refs[10:12]
    tabs = refs[12:20]
    scratch = refs[20:24]
    (v, planes, own, pack, coeffs, spread, landed, pairs, mate, gathered, blocks, rotation_ref, left, rotated, local_sem,
     a_send, a_recv, v_send, v_recv, b_send, b_recv, c_send, c_recv) = refs[24:]
    band = lax.axis_index("band")
    grid = lax.axis_index("grid")
    z_hi, y, core, chip = band // 8, (band // 2) % 4, band % 2, band // 2
    z_lo, x = grid // 4, grid % 4
    sibling = (z_hi * 8 + y * 2 + 1 - core, grid)

    def z_step(step, other=0):
        z = (z_hi * 2 + z_lo + step) % 8
        return ((z // 2) * 8 + y * 2 + (core + other) % 2, (1 - z_lo) * 4 + x)

    def x_step(step):
        return (band, z_lo * 4 + (x + step) % 4)

    def y_step(step):
        return (z_hi * 8 + ((y + step) % 4) * 2 + core, grid)

    def remote(src, dst, send, recv, to):
        return pltpu.make_async_remote_copy(
            src_ref=src, dst_ref=dst, send_sem=send, recv_sem=recv, device_id=to, device_id_type=MESH
        )

    sources = (v_hbm, tables_hbm[6], tables_hbm[7], x_hbm, rotation_hbm) + tuple(tables_hbm[:6])
    targets = (v_ref, tabs[6], tabs[7], x_ref, rotation_ref) + tuple(tabs[:6])
    fetches = [
        pltpu.make_async_copy(src, dst, local_sem.at[i])
        for i, (src, dst) in enumerate(zip(sources, targets))
    ]
    for fetch in fetches:
        fetch.start()

    barrier = pltpu.get_barrier_semaphore()

    def greet(to):
        pl.semaphore_signal(barrier, inc=1, device_id=to, device_id_type=MESH)

    @pl.loop(1, SHARDS)
    def _(d):
        greet((band, (grid + d) % SHARDS))
        greet((sibling[0], (grid + d) % SHARDS))

    @pl.loop(1, CHIPS)
    def _(d):
        greet((((chip + d) % CHIPS) * 2 + core, grid))

    greet(sibling)
    for other in range(2):
        greet(z_step(1, other))
        greet(z_step(7, other))

    for fetch in fetches[:3]:
        fetch.wait()
    fit_potential(v_ref, tabs, planes, own)
    for column in range(2):
        v[column, grid] = own[192 * column : 192 * column + 192]
    pl.semaphore_wait(barrier, 2 * (SHARDS - 1) + CHIPS - 1 + 5)

    def rows_of(ref, block, size):
        return ref.at[pl.ds(pl.multiple_of(block * size, size), size), :]

    def bring(to, block, slot):
        return remote(
            rows_of(pack, block, 32), rows_of(coeffs, slot, 32), a_send.at[0], a_recv.at[0], (band, to)
        )

    def all_rows(ref, sem):
        count = pl.ds(0, 224 if sem == 0 else 240)
        return remote(ref.at[count, :], ref.at[count, :], a_send.at[sem], a_recv.at[sem], sibling)

    near = [z_lo * 4 + (x + s) % 4 for s in (0, 3, 1, 2)]
    far = [(1 - z_lo) * 4 + (x + s) % 4 for s in (0, 3, 1, 2)]

    def v_copy(sem, shard, to, part=None, column=core):
        rows = pl.ds(0, 192) if part is None else pl.ds(96 * part, 96)
        ref = v.at[column, shard, rows, :]
        return remote(ref, ref, v_send.at[sem], v_recv.at[sem], to)

    sent = []

    def v_go(*where):
        copy = v_copy(*where)
        copy.start()
        sent.append(copy)

    def along_z(s, part):
        v_go(6 + 2 * s + part, near[s], z_step(7 if part else 1), part)

    def from_x(sem, s, part):
        v_copy(sem, near[s], sibling, part).wait_recv()
        along_z(s, part)

    def last_along_z(part):
        v_copy(4 + part, near[3], sibling, part).wait_recv()
        along_z(3, part)
        v_go(20 + part, near[3], z_step(7 if part else 1, 1), part)

    def from_z(s):
        for part in range(2):
            v_copy(6 + 2 * s + part, far[s], sibling, part).wait_recv()
        v_go(17 + s, far[s], sibling)

    v_go(0, near[0], x_step(1), 0)
    v_go(3, near[0], x_step(3), 1)
    v_go(1, near[0], x_step(1), 1)
    v_go(2, near[0], x_step(3), 0)
    along_z(0, 0)
    along_z(0, 1)
    fetches[3].wait()
    for r in range(32):
        pack[pl.ds(r, 8, stride=32), :] = x_ref[:, 128 * r : 128 * r + 128]
    center = (lower[0] + upper[0]) * 0.5
    inverse = 1.0 / ((upper[0] - lower[0]) * 0.5)
    for fetch in fetches[4:]:
        fetch.wait()
    rh, rl = split(rotation_ref[...].T)
    left[...] = jnp.concatenate([rh, rl, rh, rl], 1)
    from_x(0, 1, 0)
    v_go(4, near[1], x_step(1), 0)
    from_x(3, 2, 1)
    v_go(5, near[2], x_step(3), 1)
    for d in range(1, SHARDS):
        to = (grid + d) % SHARDS
        bring(to, to, grid).start()
    rows_of(coeffs, grid, 32)[...] = rows_of(pack, grid, 32)[...]
    from_x(1, 1, 1)
    v_go(14, near[1], sibling)
    from_x(2, 2, 0)
    v_go(15, near[2], sibling)
    from_z(0)
    last_along_z(0)
    last_along_z(1)
    v_go(16, near[3], sibling)
    from_z(1)
    from_z(2)
    all_rows(coeffs, 0).wait_recv()
    c = jnp.concatenate([coeffs[pl.ds(k8, 32, stride=8), :] for k8 in range(8)], 1)
    expand_rows(c, tabs, scratch)
    for part in range(2):
        v_copy(12 + part, far[3], sibling, part).wait_recv()
    cross_planes(core, v, tabs, scratch)
    for s in range(1, 4):
        v_copy(13 + s, near[s], sibling, None, 1 - core).wait_recv()
    for s in range(3):
        v_copy(17 + s, far[s], sibling, None, 1 - core).wait_recv()
    for part in range(2):
        v_copy(20 + part, far[3], sibling, part, 1 - core).wait_recv()
    cross_planes(1 - core, v, tabs, scratch)
    shift = kinetic_plane() - center
    first = (shift * c + contract_rows(tabs, scratch)) * inverse
    expand_rows(first, tabs, scratch)
    cross_planes(0, v, tabs, scratch)
    cross_planes(1, v, tabs, scratch)
    second = shift * first + contract_rows(tabs, scratch)
    out = (2.0 * inverse) * second - c
    all_rows(coeffs, 0).wait_send()
    for k8 in range(8):
        pack[pl.ds(k8, 32, stride=8), :] = out[:, 128 * k8 : 128 * k8 + 128]
    for k in range(2):
        spread[pl.ds(128 * k, 128), :] = pack[pl.ds(k, 128, stride=2), :]

    def bring_back(to, other):
        k = 1 - core if other else core
        return remote(
            rows_of(spread, k * 8 + to, 16), rows_of(landed, core * 8 + grid, 16),
            a_send.at[1], a_recv.at[1], (chip * 2 + k, to),
        )

    for d in range(1, SHARDS):
        for other in range(2):
            bring_back((grid + d) % SHARDS, other).start()
    bring_back(grid, 1).start()
    rows_of(landed, core * 8 + grid, 16)[...] = rows_of(spread, core * 8 + grid, 16)[...]
    for copy in sent:
        copy.wait_send()
    all_rows(landed, 1).wait_recv()
    for k in range(2):
        for i in range(CHIPS):
            pairs[i, k] = landed[pl.ds(128 * k + i, 8, stride=16), :]

    for dz, dy in sorted(
        ((dz, dy) for dz in range(4) for dy in range(4) if dz + dy),
        key=lambda d: -2 * min(d[0], 4 - d[0]) - min(d[1], 4 - d[1]),
    ):
        to = (z_hi + dz) % 4 * 4 + (y + dy) % 4
        remote(pairs.at[to], blocks.at[chip], b_send.at[1], b_recv.at[1], (to * 2 + core, grid)).start()

    blocks[chip] = pairs[chip]
    swap = remote(pairs.at[:, 1 - core], mate, b_send.at[0], b_recv.at[0], sibling)
    swap.start()
    all_chips = remote(
        pairs.at[pl.ds(0, CHIPS - 1)], blocks.at[pl.ds(0, CHIPS - 1)], b_send.at[1], b_recv.at[1], sibling
    )
    all_chips.wait_recv()
    for s in range(STEPS):
        gathered[band, pl.ds(8 * s, 8), :] = blocks[owners[s] // 2, owners[s] % 2]

    def c_copy(sem, index, to):
        ref = gathered.at[index]
        return remote(ref, ref, c_send, c_recv.at[sem], (to, grid))

    def index_of(dz, dy):
        return ((z_hi + 4 - dz) % 4) * 8 + ((y + 4 - dy) % 4) * 2 + core

    def deliver(dz, dy):
        c_copy(16 + 4 * dz + dy, index_of(dz, dy), sibling[0]).start()

    def along_z_hi(dz):
        c_copy(dz, band, ((z_hi + dz) % 4) * 8 + band % 8).start()

    def along_y(dz):
        mine = index_of(dz, 0)
        for dy in (1, 3, 2):
            c_copy(4 + 3 * dz + dy - 1, mine, z_hi * 8 + ((y + dy) % 4) * 2 + core).start()
        deliver(dz, 0)

    def from_y(dz):
        for dy in (1, 3, 2):
            c_copy(4 + 3 * dz + dy - 1, index_of(dz, dy), sibling[0]).wait_recv()
            deliver(dz, dy)

    def rotate(dz):
        for dy in range(4):
            twin = index_of(dz, dy) + 1 - 2 * core
            c_copy(16 + 4 * dz + dy, twin, sibling[0]).wait_recv()
        level = (z_hi + 4 - dz) % 4
        ah, al = split(jnp.concatenate([gathered[level * 8 + i] for i in range(8)], 1))
        at = pl.ds(pl.multiple_of(level * 1024, 1024), 1024)
        rotated[:, at] = dot(left[...], jnp.concatenate([ah, ah, al, al], 0))
        return pltpu.make_async_copy(rotated.at[:, at], residents.at[:, at], local_sem.at[1 + dz])

    along_z_hi(1)
    along_z_hi(3)
    along_y(0)
    along_z_hi(2)
    for dz in (1, 3):
        c_copy(dz, index_of(dz, 0), sibling[0]).wait_recv()
        along_y(dz)
    swap.wait_recv()
    for i in range(CHIPS):
        x_ref[:, pl.ds(pl.multiple_of(256 * i + 128 * core, 128), 128)] = pairs[i, core]
        x_ref[:, pl.ds(pl.multiple_of(256 * i + 128 - 128 * core, 128), 128)] = mate[i]
    write = pltpu.make_async_copy(x_ref, filtered, local_sem.at[0])
    write.start()
    from_y(0)
    c_copy(2, index_of(2, 0), sibling[0]).wait_recv()
    along_y(2)
    writes = [write]

    def finish(dz):
        writes.append(rotate(dz))
        writes[-1].start()

    finish(0)
    from_y(1)
    from_y(3)
    finish(1)
    from_y(2)
    finish(3)
    finish(2)
    all_chips.wait_send()
    all_rows(landed, 1).wait_send()
    swap.wait_send()
    every = pl.ds(0, GROUPS - 1)
    remote(gathered.at[every], gathered.at[every], c_send, c_recv.at[0], sibling).wait_send()
    for copy in writes:
        copy.wait()


SMEM = pl.BlockSpec(memory_space=pltpu.SMEM)
ANY = pl.BlockSpec(memory_space=pl.ANY)
FILTER = pl.pallas_call(
    filter_kernel,
    out_shape=(
        jax.ShapeDtypeStruct((8, 4096), F32),
        jax.ShapeDtypeStruct((192, 4096), F32),
    ),
    in_specs=[ANY] * 3 + [SMEM] * 3 + [ANY] * 8,
    out_specs=(ANY, ANY),
    scratch_shapes=[
        pltpu.VMEM((8, 4096), F32),
        pltpu.VMEM((12, 9216), F32),
        pltpu.VMEM((64, 128), BF16),
        pltpu.VMEM((128, 512), BF16),
        pltpu.VMEM((192, 256), BF16),
        pltpu.VMEM((128, 192), BF16),
        pltpu.VMEM((256, 256), BF16),
        pltpu.VMEM((64, 128), BF16),
        pltpu.VMEM((384, 512), BF16),
        pltpu.VMEM((64, 384), BF16),
    ] + H_SCRATCH + [
        pltpu.VMEM((2, SHARDS, 192, 128), F32),
        pltpu.VMEM((2, 384, 128), F32),
        pltpu.VMEM((384, 128), F32),
        pltpu.VMEM((256, 128), F32),
        pltpu.VMEM((256, 128), F32),
        pltpu.VMEM((256, 128), F32),
        pltpu.VMEM((256, 128), F32),
        pltpu.VMEM((CHIPS, 2, 8, 128), F32),
        pltpu.VMEM((CHIPS, 8, 128), F32),
        pltpu.VMEM((GROUPS, 64, 128), F32),
        pltpu.VMEM((CHIPS, 2, 8, 128), F32),
        pltpu.VMEM((64, 192), F32),
        pltpu.VMEM((192, 256), BF16),
        pltpu.VMEM((192, 4096), F32),
        pltpu.SemaphoreType.DMA((11,)),
        pltpu.SemaphoreType.DMA((2,)),
        pltpu.SemaphoreType.DMA((2,)),
        pltpu.SemaphoreType.DMA((22,)),
        pltpu.SemaphoreType.DMA((22,)),
        pltpu.SemaphoreType.DMA((2,)),
        pltpu.SemaphoreType.DMA((2,)),
        pltpu.SemaphoreType.DMA,
        pltpu.SemaphoreType.DMA((32,)),
    ],
    compiler_params=pltpu.CompilerParams(
        collective_id=0, has_side_effects=True, vmem_limit_bytes=VMEM_LIMIT
    ),
    name="filter",
)


def write_kernel(filtered, residents, filtered_out, residents_out, block, rows, in_sem, out_sem):
    parts = [(filtered, block, filtered_out)]
    for i in range(8):
        at = pl.ds(24 * i, 24)
        parts.append((residents.at[at, :], rows.at[at, :], residents_out.at[at, :]))
    reads = [pltpu.make_async_copy(a, b, in_sem.at[i]) for i, (a, b, _) in enumerate(parts)]
    writes = [pltpu.make_async_copy(b, c, out_sem.at[i]) for i, (_, b, c) in enumerate(parts)]
    for read in reads:
        read.start()
    for read, write in zip(reads, writes):
        read.wait()
        write.start()
    for write in writes:
        write.wait()


WRITE = pl.pallas_call(
    write_kernel,
    out_shape=(
        jax.ShapeDtypeStruct((8, 4096), F32),
        jax.ShapeDtypeStruct((192, 4096), F32),
    ),
    in_specs=[ANY] * 2,
    out_specs=(ANY, ANY),
    scratch_shapes=[
        pltpu.VMEM((8, 4096), F32),
        pltpu.VMEM((192, 4096), F32),
        pltpu.SemaphoreType.DMA((9,)),
        pltpu.SemaphoreType.DMA((9,)),
    ],
    compiler_params=pltpu.CompilerParams(vmem_limit_bytes=VMEM_LIMIT),
    name="write",
)


def body(block_coeffs, potential, lower_edge, upper_edge, rotation, owners):
    consts = [jnp.asarray(t) for t in tables()]
    coefficients = rotation.transpose(0, 2, 1).reshape(64, 192)
    return tuple(
        WRITE(*FILTER(block_coeffs, potential, coefficients, lower_edge, upper_edge, owners, *consts))
    )


def solution(mesh):
    return jax.shard_map(
        body,
        mesh=mesh,
        in_specs=(P("band", "grid"), P("grid", None), P(), P(), P(None, "band", None), P()),
        out_specs=(P("band", "grid"), P("band", "grid")),
        check_vma=False,
    )
```

```python
import functools

import jax
import jax.numpy as jnp
import ml_dtypes
import numpy as np
from jax import lax
from jax.experimental import pallas as pl
from jax.experimental.pallas import tpu as pltpu
from jax.sharding import PartitionSpec as P

NG = 96
KEEP = 32
NS = 64
SHARDS = 8
BANDS = 8
GROUPS = 32
CHIPS = 16
STEPS = 8
CORNERS = (2,)
edge_energy = 1.3

F32 = jnp.float32
BF16 = jnp.bfloat16
MESH = pl.DeviceIdType.MESH
VMEM_LIMIT = 58 << 20


def split_table(table):
    hi = table.astype(ml_dtypes.bfloat16)
    lo = (table - hi.astype(np.float64)).astype(ml_dtypes.bfloat16)
    return hi, lo


def hartley_table():
    ordinal = np.arange(KEEP)
    frequency = np.where(ordinal < KEEP // 2, ordinal, ordinal + NG - KEEP)
    angle = (np.arange(NG)[:, None] * frequency[None, :] % NG) * (2.0 * np.pi / NG)
    return (np.cos(angle) + np.sin(angle)) / np.sqrt(float(NG))


def fine_points():
    return np.arange(NG) * (2.0 * np.pi / NG)


def short_points():
    return (np.arange(NS) + 0.5) * (2.0 * np.pi / NS)


def short_table():
    ordinal = np.arange(KEEP)
    signed = np.where(ordinal < KEEP // 2, ordinal, ordinal - KEEP)
    angle = short_points()[:, None] * signed[None, :]
    return (np.cos(angle) + np.sin(angle)) / np.sqrt(float(NG))


def resample_table():
    gap = short_points()[:, None] - fine_points()[None, :]
    table = 1.0 + 2.0 * sum(np.cos(f * gap) for f in range(1, KEEP))
    table = table + np.sin(KEEP * short_points())[:, None] * np.sin(KEEP * fine_points())[None, :]
    return table / NS


def four_blocks(table):
    return np.kron(np.eye(4), table.astype(np.float32)).astype(table.dtype)


def tables():
    hi, lo = split_table(hartley_table())
    short_hi, short_lo = split_table(short_table())
    fit_hi, fit_lo = split_table(resample_table())
    zero = np.zeros((), ml_dtypes.bfloat16)
    order = np.array([4 * (r % 16) + r // 16 for r in range(NS)])
    y_syn = np.concatenate([short_hi, short_lo, short_hi, short_lo], 1)[order]
    z_syn = np.concatenate([four_blocks(short_hi.T), four_blocks(short_lo.T)], 1)
    stacked = np.concatenate([hi, lo, hi, lo], 1)
    x_syn = np.full((SHARDS, 2, 12, 2, 128), zero)
    for half in range(2):
        x_syn[:, half, :, half] = stacked.reshape(SHARDS, 12, 128)
    x_syn = x_syn.reshape(192, 256)
    parts = []
    for t in (hi, lo):
        part = np.full((2, KEEP, SHARDS, 2, 12), zero)
        for half in range(2):
            part[half, :, :, half, :] = t.T.reshape(KEEP, SHARDS, 12)
        parts.append(part.reshape(64, 192))
    x_ana = np.concatenate(parts, 0)
    z_ana = np.concatenate([four_blocks(short_hi), four_blocks(short_lo)], 1)
    y_ana = np.concatenate([np.concatenate([t[order].T] * 2, 1) for t in (short_hi, short_lo)], 0)
    z_fit = np.concatenate([four_blocks(fit_hi.T), four_blocks(fit_lo.T)], 1)
    rows = np.array([2 * (r % 32) + r // 32 for r in range(NS)])
    columns = np.array([4 * (r % 24) + r // 24 for r in range(NG)])
    y_fit = np.concatenate([t[rows][:, columns] for t in (fit_hi, fit_lo, fit_hi, fit_lo)], 1)
    return y_syn, z_syn, x_syn, x_ana, z_ana, y_ana, z_fit, y_fit


def kinetic_plane():
    def square(k):
        signed = jnp.where(k < KEEP // 2, k, k - KEEP)
        return (signed * signed).astype(F32) * (1.0 / (KEEP // 2) ** 2)

    ky = lax.broadcasted_iota(jnp.int32, (KEEP, KEEP * KEEP), 0)
    lane = lax.broadcasted_iota(jnp.int32, (KEEP, KEEP * KEEP), 1)
    return edge_energy * (square(ky) + square(lane // KEEP) + square(lane % KEEP))


def split(x):
    hi = x.astype(BF16)
    return hi, (x - hi.astype(F32)).astype(BF16)


def dot(a, b):
    return jnp.dot(a, b, preferred_element_type=F32)


def swap_groups(parts):
    lane = lax.broadcasted_iota(jnp.int32, parts[0].shape, 1)
    low = lane < 64
    even = lane % 64 < 32
    half = [None] * 4
    for j in range(2):
        half[j] = jnp.where(low, parts[j], pltpu.roll(parts[j + 2], 64, 1))
        half[j + 2] = jnp.where(low, pltpu.roll(parts[j], 64, 1), parts[j + 2])
    out = []
    for a, b in ((half[0], half[1]), (half[2], half[3])):
        out.append(jnp.where(even, a, pltpu.roll(b, 32, 1)))
        out.append(jnp.where(even, pltpu.roll(a, 96, 1), b))
    return out


def twofold(a, table, width):
    ah, al = split(a)
    wide = dot(ah, table[...])
    return wide[:, :width] + wide[:, width:] + dot(al, table[:, :width])


def fit_potential(v_ref, tabs, planes, own):
    z_fit, y_fit = tabs[6:]
    lane = lax.broadcasted_iota(jnp.int32, (32, 128), 1)
    low = lane < 64
    blank = jnp.zeros((4, 384), F32)
    blocks = []
    for c in range(24):
        blocks += [v_ref[:, 384 * c : 384 * c + 384], blank]
    fit = twofold(jnp.concatenate(blocks, 0), z_fit, 256)
    for tile in range(2):
        planes[tile] = fit[:, 128 * tile : 128 * tile + 128]
    columns = []
    for n in range(0, 12, 2):
        parts = []
        for j in range(4):
            a = planes[j // 2, pl.ds(n, 24, stride=16), :]
            b = planes[j // 2, pl.ds(n + 1, 24, stride=16), :]
            if j % 2 == 0:
                parts.append(jnp.where(low[:24], a, pltpu.roll(b, 64, 1)))
            else:
                parts.append(jnp.where(low[:24], pltpu.roll(a, 64, 1), b))
        columns.append(jnp.concatenate(parts, 0))
    hi, lo = split(jnp.concatenate(columns, 1))
    fit = dot(y_fit[...], jnp.concatenate([hi, hi, lo, lo], 0))
    for n in range(0, 12, 2):
        even, odd = fit[:32, 64 * n : 64 * n + 128], fit[32:, 64 * n : 64 * n + 128]
        first = jnp.where(low, even, pltpu.roll(odd, 64, 1))
        second = jnp.where(low, pltpu.roll(even, 64, 1), odd)
        for p, plane in ((n, first), (n + 1, second)):
            for half in range(2):
                for column in range(2):
                    t = 16 * half + 8 * column
                    own[pl.ds(192 * column + 12 * half + p, 8, stride=24), :] = plane[t : t + 8]


def expand_rows(c, tabs, scratch):
    y_syn, z_syn = tabs[:2]
    d1, d2h, d2l, _ = scratch
    ch, cl = split(c)
    along_y = dot(y_syn[...], jnp.concatenate([ch, ch, cl, cl], 0))
    for k8 in range(8):
        cols = slice(128 * k8, 128 * k8 + 128)
        parts = swap_groups([along_y[16 * j : 16 * j + 16, cols] for j in range(4)])
        for m in range(4):
            d1[pl.ds((4 * k8 + m) * 16, 16), :] = parts[m]
    for i in range(2):
        rows = jnp.concatenate([d1[pl.ds(8 * i + j, 32, stride=16), :] for j in range(8)], 0)
        dh, dl = split(twofold(rows, z_syn, 256))
        d2h[pl.ds(256 * i, 256), :] = dh
        d2l[pl.ds(256 * i, 256), :] = dl


def cross_planes(column, v, tabs, scratch):
    _, _, x_syn, x_ana = tabs[:4]
    _, d2h, d2l, bz = scratch

    def plane_step(i, carry):
        q = column * 4 + i
        r0 = pl.multiple_of(q * 32, 32)
        r1 = pl.multiple_of(q * 32 + 256, 32)
        h0, l0 = d2h[pl.ds(r0, 32), :], d2l[pl.ds(r0, 32), :]
        h1, l1 = d2h[pl.ds(r1, 32), :], d2l[pl.ds(r1, 32), :]
        field = dot(x_syn[...], jnp.concatenate([h0, h0, l0, l0, h1, h1, l1, l1], 0))
        tiles = [
            v[column, :, pl.ds(pl.multiple_of(48 * i + 24 * j, 8), 24), :].reshape(192, 128)
            for j in range(2)
        ]
        wh, wl = split(field * jnp.concatenate(tiles, 1))
        first = dot(x_ana[...], wh)
        back = first[:64] + first[64:] + dot(x_ana[pl.ds(0, 64), :], wl)
        bz[pl.ds(r0, 32), :] = back[:32]
        bz[pl.ds(r1, 32), :] = back[32:]
        return carry

    lax.fori_loop(0, 4, plane_step, 0, unroll=True)


def contract_rows(tabs, scratch):
    z_ana, y_ana = tabs[4:6]
    d1, _, _, bz = scratch
    for i in range(2):
        d1[pl.ds(256 * i, 256), :] = twofold(bz[pl.ds(256 * i, 256), :], z_ana, 128)
    columns = []
    for k8 in range(8):
        parts = [d1[pl.ds(4 * k8 + m, 16, stride=32), :] for m in range(4)]
        columns.append(jnp.concatenate(swap_groups(parts), 0))
    gh, gl = split(jnp.concatenate(columns, 1))
    back = dot(y_ana[...], jnp.concatenate([gh, gl], 0))
    return back[:32] + back[32:]


H_SCRATCH = [
    pltpu.VMEM((512, 128), F32),
    pltpu.VMEM((512, 256), BF16),
    pltpu.VMEM((512, 256), BF16),
    pltpu.VMEM((512, 256), F32),
]


def filter_kernel(x_hbm, v_hbm, rotation_hbm, lower, upper, owners, *refs):
    tables_hbm = refs[:8]
    filtered, residents = refs[8:10]
    x_ref, v_ref = refs[10:12]
    tabs = refs[12:20]
    scratch = refs[20:24]
    (v, planes, own, pack, coeffs, spread, landed, pairs, mate, gathered, blocks, relay, rotation_ref, left, rotated, local_sem,
     a_send, a_recv, v_send, v_recv, b_send, b_recv, c_send, c_recv, news) = refs[24:]
    band = lax.axis_index("band")
    grid = lax.axis_index("grid")
    z_hi, y, core, chip = band // 8, (band // 2) % 4, band % 2, band // 2
    z_lo, x = grid // 4, grid % 4
    sibling = (z_hi * 8 + y * 2 + 1 - core, grid)

    def z_step(step, other=0):
        z = (z_hi * 2 + z_lo + step) % 8
        return ((z // 2) * 8 + y * 2 + (core + other) % 2, (1 - z_lo) * 4 + x)

    def x_step(step):
        return (band, z_lo * 4 + (x + step) % 4)

    def y_step(step):
        return (z_hi * 8 + ((y + step) % 4) * 2 + core, grid)

    def remote(src, dst, send, recv, to):
        return pltpu.make_async_remote_copy(
            src_ref=src, dst_ref=dst, send_sem=send, recv_sem=recv, device_id=to, device_id_type=MESH
        )

    sources = (v_hbm, tables_hbm[6], tables_hbm[7], x_hbm, rotation_hbm) + tuple(tables_hbm[:6])
    targets = (v_ref, tabs[6], tabs[7], x_ref, rotation_ref) + tuple(tabs[:6])
    fetches = [
        pltpu.make_async_copy(src, dst, local_sem.at[i])
        for i, (src, dst) in enumerate(zip(sources, targets))
    ]
    for fetch in fetches:
        fetch.start()

    barrier = pltpu.get_barrier_semaphore()
    neighbours = [z_step(step, other) for step in (1, 7) for other in range(2)]
    neighbours += [x_step(1), x_step(3), y_step(1), y_step(3), sibling]
    for to in neighbours:
        pl.semaphore_signal(barrier, inc=1, device_id=to, device_id_type=MESH)

    def tell(turn):
        for to in (y_step(1), y_step(3)) if turn == 0 else (z_step(1), z_step(7)):
            pl.semaphore_signal(news.at[turn], inc=1, device_id=to, device_id_type=MESH)

    def hear(turn):
        pl.semaphore_wait(news.at[turn], 2)

    for fetch in fetches[:3]:
        fetch.wait()
    fit_potential(v_ref, tabs, planes, own)
    for column in range(2):
        v[column, grid] = own[192 * column : 192 * column + 192]
    pl.semaphore_wait(barrier, len(neighbours))
    tell(0)

    def rows_of(ref, block, size):
        return ref.at[pl.ds(pl.multiple_of(block * size, size), size), :]

    def bring(to, block, slot):
        return remote(
            rows_of(pack, block, 32), rows_of(coeffs, slot, 32), a_send.at[0], a_recv.at[0], (band, to)
        )

    def all_rows(ref, sem):
        count = pl.ds(0, 224 if sem == 0 else 240)
        return remote(ref.at[count, :], ref.at[count, :], a_send.at[sem], a_recv.at[sem], sibling)

    near = [z_lo * 4 + (x + s) % 4 for s in (0, 3, 1, 2)]
    far = [(1 - z_lo) * 4 + (x + s) % 4 for s in (0, 3, 1, 2)]

    def v_copy(sem, shard, to, part=None, column=core):
        rows = pl.ds(0, 192) if part is None else pl.ds(96 * part, 96)
        ref = v.at[column, shard, rows, :]
        return remote(ref, ref, v_send.at[sem], v_recv.at[sem], to)

    sent = []

    def v_go(*where):
        copy = v_copy(*where)
        copy.start()
        sent.append(copy)

    def along_z(s, part):
        v_go(6 + 2 * s + part, near[s], z_step(7 if part else 1), part)

    def from_x(sem, s, part):
        v_copy(sem, near[s], sibling, part).wait_recv()
        along_z(s, part)

    def last_along_z(part):
        v_copy(4 + part, near[3], sibling, part).wait_recv()
        along_z(3, part)
        v_go(20 + part, near[3], z_step(7 if part else 1, 1), part)

    def from_z(s):
        for part in range(2):
            v_copy(6 + 2 * s + part, far[s], sibling, part).wait_recv()
        v_go(17 + s, far[s], sibling)

    v_go(0, near[0], x_step(1), 0)
    v_go(3, near[0], x_step(3), 1)
    v_go(1, near[0], x_step(1), 1)
    v_go(2, near[0], x_step(3), 0)
    along_z(0, 0)
    along_z(0, 1)
    fetches[3].wait()
    for r in range(32):
        pack[pl.ds(r, 8, stride=32), :] = x_ref[:, 128 * r : 128 * r + 128]
    partner = (1 - z_lo) * 4 + x
    by_z = remote(
        rows_of(pack, (1 - z_lo) * 4 + (x + 2) % 4, 32), relay, a_send.at[2], a_recv.at[2], (band, partner)
    )
    by_z.start()
    center = (lower[0] + upper[0]) * 0.5
    inverse = 1.0 / ((upper[0] - lower[0]) * 0.5)
    for fetch in fetches[4:]:
        fetch.wait()
    rh, rl = split(rotation_ref[...].T)
    left[...] = jnp.concatenate([rh, rl, rh, rl], 1)
    from_x(0, 1, 0)
    v_go(4, near[1], x_step(1), 0)
    from_x(3, 2, 1)
    v_go(5, near[2], x_step(3), 1)
    hear(0)
    tell(1)
    for dz, dx in ((0, 2), (1, 1), (1, 3), (1, 0), (0, 1), (0, 3)):
        to = (z_lo + dz) % 2 * 4 + (x + dx) % 4
        bring(to, to, grid).start()
    rows_of(coeffs, grid, 32)[...] = rows_of(pack, grid, 32)[...]
    by_z.wait_recv()
    remote(
        relay, rows_of(coeffs, partner, 32), a_send.at[0], a_recv.at[0], (band, z_lo * 4 + (x + 2) % 4)
    ).start()
    from_x(1, 1, 1)
    v_go(14, near[1], sibling)
    from_x(2, 2, 0)
    v_go(15, near[2], sibling)
    from_z(0)
    hear(1)
    last_along_z(0)
    last_along_z(1)
    v_go(16, near[3], sibling)
    tell(2)
    from_z(1)
    from_z(2)
    all_rows(coeffs, 0).wait_recv()
    c = jnp.concatenate([coeffs[pl.ds(k8, 32, stride=8), :] for k8 in range(8)], 1)
    expand_rows(c, tabs, scratch)
    for part in range(2):
        v_copy(12 + part, far[3], sibling, part).wait_recv()
    hear(2)
    tell(3)
    cross_planes(core, v, tabs, scratch)
    for s in range(1, 4):
        v_copy(13 + s, near[s], sibling, None, 1 - core).wait_recv()
    for s in range(3):
        v_copy(17 + s, far[s], sibling, None, 1 - core).wait_recv()
    for part in range(2):
        v_copy(20 + part, far[3], sibling, part, 1 - core).wait_recv()
    cross_planes(1 - core, v, tabs, scratch)
    shift = kinetic_plane() - center
    first = (shift * c + contract_rows(tabs, scratch)) * inverse
    hear(3)
    tell(4)
    expand_rows(first, tabs, scratch)
    cross_planes(0, v, tabs, scratch)
    cross_planes(1, v, tabs, scratch)
    second = shift * first + contract_rows(tabs, scratch)
    out = (2.0 * inverse) * second - c
    all_rows(coeffs, 0).wait_send()
    by_z.wait_send()
    for k8 in range(8):
        pack[pl.ds(k8, 32, stride=8), :] = out[:, 128 * k8 : 128 * k8 + 128]
    for k in range(2):
        spread[pl.ds(128 * k, 128), :] = pack[pl.ds(k, 128, stride=2), :]

    def bring_back(to, other):
        k = 1 - core if other else core
        return remote(
            rows_of(spread, k * 8 + to, 16), rows_of(landed, core * 8 + grid, 16),
            a_send.at[1], a_recv.at[1], (chip * 2 + k, to),
        )

    for d in range(1, SHARDS):
        for other in range(2):
            bring_back((grid + d) % SHARDS, other).start()
    bring_back(grid, 1).start()
    rows_of(landed, core * 8 + grid, 16)[...] = rows_of(spread, core * 8 + grid, 16)[...]
    for copy in sent:
        copy.wait_send()
    all_rows(landed, 1).wait_recv()
    for k in range(2):
        for i in range(CHIPS):
            pairs[i, k] = landed[pl.ds(128 * k + i, 8, stride=16), :]

    hear(4)

    for dz, dy in sorted(
        ((dz, dy) for dz in range(4) for dy in range(4) if dz + dy),
        key=lambda d: -2 * min(d[0], 4 - d[0]) - min(d[1], 4 - d[1]),
    ):
        to = (z_hi + dz) % 4 * 4 + (y + dy) % 4
        remote(pairs.at[to], blocks.at[chip], b_send.at[1], b_recv.at[1], (to * 2 + core, grid)).start()

    blocks[chip] = pairs[chip]
    swap = remote(pairs.at[:, 1 - core], mate, b_send.at[0], b_recv.at[0], sibling)
    swap.start()
    all_chips = remote(
        pairs.at[pl.ds(0, CHIPS - 1)], blocks.at[pl.ds(0, CHIPS - 1)], b_send.at[1], b_recv.at[1], sibling
    )
    all_chips.wait_recv()
    for s in range(STEPS):
        gathered[band, pl.ds(8 * s, 8), :] = blocks[owners[s] // 2, owners[s] % 2]

    def c_copy(sem, index, to):
        ref = gathered.at[index]
        return remote(ref, ref, c_send, c_recv.at[sem], (to, grid))

    def index_of(dz, dy):
        return ((z_hi + 4 - dz) % 4) * 8 + ((y + 4 - dy) % 4) * 2 + core

    def deliver(dz, dy):
        c_copy(16 + 4 * dz + dy, index_of(dz, dy), sibling[0]).start()

    def along_z_hi(dz):
        c_copy(dz, band, ((z_hi + dz) % 4) * 8 + band % 8).start()

    def along_y(dz):
        mine = index_of(dz, 0)
        for dy in (1, 3) if dz in CORNERS else (2, 1, 3):
            c_copy(4 + 3 * dz + dy - 1, mine, z_hi * 8 + ((y + dy) % 4) * 2 + core).start()
        deliver(dz, 0)

    def from_y(dz):
        for dy in (1, 3, 2):
            c_copy(4 + 3 * dz + dy - 1, index_of(dz, dy), sibling[0]).wait_recv()
            if dz == 0 and dy == 2:
                for corner in CORNERS:
                    c_copy(
                        4 + 3 * corner + 1, index_of(0, 2), ((z_hi + corner) % 4) * 8 + band % 8
                    ).start()
            deliver(dz, dy)

    def rotate(dz):
        for dy in range(4):
            twin = index_of(dz, dy) + 1 - 2 * core
            c_copy(16 + 4 * dz + dy, twin, sibling[0]).wait_recv()
        level = (z_hi + 4 - dz) % 4
        return columns_of(level * 8, 8, 1 + dz)

    def rotate_pair(dz, dy):
        twin = index_of(dz, dy) + 1 - 2 * core
        c_copy(16 + 4 * dz + dy, twin, sibling[0]).wait_recv()
        return columns_of(twin // 2 * 2, 2, 3 if dy == 0 else 4 + dy)

    def columns_of(first, count, sem):
        ah, al = split(jnp.concatenate([gathered[first + i] for i in range(count)], 1))
        at = pl.ds(pl.multiple_of(first * 128, 256), 128 * count)
        rotated[:, at] = dot(left[...], jnp.concatenate([ah, ah, al, al], 0))
        write = pltpu.make_async_copy(rotated.at[:, at], residents.at[:, at], local_sem.at[sem])
        write.start()
        writes.append(write)

    along_z_hi(1)
    along_z_hi(3)
    along_y(0)
    along_z_hi(2)
    for dz in (1, 3):
        c_copy(dz, index_of(dz, 0), sibling[0]).wait_recv()
        along_y(dz)
    swap.wait_recv()
    for i in range(CHIPS):
        x_ref[:, pl.ds(pl.multiple_of(256 * i + 128 * core, 128), 128)] = pairs[i, core]
        x_ref[:, pl.ds(pl.multiple_of(256 * i + 128 - 128 * core, 128), 128)] = mate[i]
    write = pltpu.make_async_copy(x_ref, filtered, local_sem.at[0])
    write.start()
    from_y(0)
    c_copy(2, index_of(2, 0), sibling[0]).wait_recv()
    along_y(2)
    writes = [write]
    rotate(0)
    from_y(1)
    from_y(3)
    rotate(1)
    from_y(2)
    rotate(3)
    for dy in (0, 1, 3, 2):
        rotate_pair(2, dy)
    all_chips.wait_send()
    all_rows(landed, 1).wait_send()
    swap.wait_send()
    every = pl.ds(0, GROUPS - 1)
    remote(gathered.at[every], gathered.at[every], c_send, c_recv.at[0], sibling).wait_send()
    for copy in writes:
        copy.wait()


SMEM = pl.BlockSpec(memory_space=pltpu.SMEM)
ANY = pl.BlockSpec(memory_space=pl.ANY)
FILTER = pl.pallas_call(
    filter_kernel,
    out_shape=(
        jax.ShapeDtypeStruct((8, 4096), F32),
        jax.ShapeDtypeStruct((192, 4096), F32),
    ),
    in_specs=[ANY] * 3 + [SMEM] * 3 + [ANY] * 8,
    out_specs=(ANY, ANY),
    scratch_shapes=[
        pltpu.VMEM((8, 4096), F32),
        pltpu.VMEM((12, 9216), F32),
        pltpu.VMEM((64, 128), BF16),
        pltpu.VMEM((128, 512), BF16),
        pltpu.VMEM((192, 256), BF16),
        pltpu.VMEM((128, 192), BF16),
        pltpu.VMEM((256, 256), BF16),
        pltpu.VMEM((64, 128), BF16),
        pltpu.VMEM((384, 512), BF16),
        pltpu.VMEM((64, 384), BF16),
    ] + H_SCRATCH + [
        pltpu.VMEM((2, SHARDS, 192, 128), F32),
        pltpu.VMEM((2, 384, 128), F32),
        pltpu.VMEM((384, 128), F32),
        pltpu.VMEM((256, 128), F32),
        pltpu.VMEM((256, 128), F32),
        pltpu.VMEM((256, 128), F32),
        pltpu.VMEM((256, 128), F32),
        pltpu.VMEM((CHIPS, 2, 8, 128), F32),
        pltpu.VMEM((CHIPS, 8, 128), F32),
        pltpu.VMEM((GROUPS, 64, 128), F32),
        pltpu.VMEM((CHIPS, 2, 8, 128), F32),
        pltpu.VMEM((32, 128), F32),
        pltpu.VMEM((64, 192), F32),
        pltpu.VMEM((192, 256), BF16),
        pltpu.VMEM((192, 4096), F32),
        pltpu.SemaphoreType.DMA((11,)),
        pltpu.SemaphoreType.DMA((3,)),
        pltpu.SemaphoreType.DMA((3,)),
        pltpu.SemaphoreType.DMA((22,)),
        pltpu.SemaphoreType.DMA((22,)),
        pltpu.SemaphoreType.DMA((2,)),
        pltpu.SemaphoreType.DMA((2,)),
        pltpu.SemaphoreType.DMA,
        pltpu.SemaphoreType.DMA((32,)),
        pltpu.SemaphoreType.REGULAR((5,)),
    ],
    compiler_params=pltpu.CompilerParams(
        collective_id=0, has_side_effects=True, vmem_limit_bytes=VMEM_LIMIT
    ),
    name="filter",
)


def write_kernel(filtered, residents, filtered_out, residents_out, block, rows, in_sem, out_sem):
    parts = [(filtered, block, filtered_out)]
    for i in range(8):
        at = pl.ds(24 * i, 24)
        parts.append((residents.at[at, :], rows.at[at, :], residents_out.at[at, :]))
    reads = [pltpu.make_async_copy(a, b, in_sem.at[i]) for i, (a, b, _) in enumerate(parts)]
    writes = [pltpu.make_async_copy(b, c, out_sem.at[i]) for i, (_, b, c) in enumerate(parts)]
    for read in reads:
        read.start()
    for read, write in zip(reads, writes):
        read.wait()
        write.start()
    for write in writes:
        write.wait()


WRITE = pl.pallas_call(
    write_kernel,
    out_shape=(
        jax.ShapeDtypeStruct((8, 4096), F32),
        jax.ShapeDtypeStruct((192, 4096), F32),
    ),
    in_specs=[ANY] * 2,
    out_specs=(ANY, ANY),
    scratch_shapes=[
        pltpu.VMEM((8, 4096), F32),
        pltpu.VMEM((192, 4096), F32),
        pltpu.SemaphoreType.DMA((9,)),
        pltpu.SemaphoreType.DMA((9,)),
    ],
    compiler_params=pltpu.CompilerParams(vmem_limit_bytes=VMEM_LIMIT),
    name="write",
)


def body(block_coeffs, potential, lower_edge, upper_edge, rotation, owners):
    consts = [jnp.asarray(t) for t in tables()]
    coefficients = rotation.transpose(0, 2, 1).reshape(64, 192)
    return tuple(
        WRITE(*FILTER(block_coeffs, potential, coefficients, lower_edge, upper_edge, owners, *consts))
    )


def solution(mesh):
    return jax.shard_map(
        body,
        mesh=mesh,
        in_specs=(P("band", "grid"), P("grid", None), P(), P(), P(None, "band", None), P()),
        out_specs=(P("band", "grid"), P("band", "grid")),
        check_vma=False,
    )
```

```python
import functools

import jax
import jax.numpy as jnp
import ml_dtypes
import numpy as np
from jax import lax
from jax.experimental import pallas as pl
from jax.experimental.pallas import tpu as pltpu
from jax.sharding import PartitionSpec as P

NG = 96
KEEP = 32
NS = 64
SHARDS = 8
BANDS = 8
GROUPS = 32
CHIPS = 16
STEPS = 8
CORNERS = (2,)
edge_energy = 1.3

F32 = jnp.float32
BF16 = jnp.bfloat16
MESH = pl.DeviceIdType.MESH
VMEM_LIMIT = 58 << 20


def split_table(table):
    hi = table.astype(ml_dtypes.bfloat16)
    lo = (table - hi.astype(np.float64)).astype(ml_dtypes.bfloat16)
    return hi, lo


def hartley_table():
    ordinal = np.arange(KEEP)
    frequency = np.where(ordinal < KEEP // 2, ordinal, ordinal + NG - KEEP)
    angle = (np.arange(NG)[:, None] * frequency[None, :] % NG) * (2.0 * np.pi / NG)
    return (np.cos(angle) + np.sin(angle)) / np.sqrt(float(NG))


def fine_points():
    return np.arange(NG) * (2.0 * np.pi / NG)


def short_points():
    return (np.arange(NS) + 0.5) * (2.0 * np.pi / NS)


def short_table():
    ordinal = np.arange(KEEP)
    signed = np.where(ordinal < KEEP // 2, ordinal, ordinal - KEEP)
    angle = short_points()[:, None] * signed[None, :]
    return (np.cos(angle) + np.sin(angle)) / np.sqrt(float(NG))


def resample_table():
    gap = short_points()[:, None] - fine_points()[None, :]
    table = 1.0 + 2.0 * sum(np.cos(f * gap) for f in range(1, KEEP))
    table = table + np.sin(KEEP * short_points())[:, None] * np.sin(KEEP * fine_points())[None, :]
    return table / NS


def block_tiles(hi, lo):
    blank = np.zeros_like(hi)
    return np.concatenate([hi, blank, blank, hi, lo, blank, blank, lo], 1)


def four_blocks(table):
    return np.kron(np.eye(4), table.astype(np.float32)).astype(table.dtype)


def tables():
    hi, lo = split_table(hartley_table())
    short_hi, short_lo = split_table(short_table())
    fit_hi, fit_lo = split_table(resample_table())
    zero = np.zeros((), ml_dtypes.bfloat16)
    order = np.array([4 * (r % 16) + r // 16 for r in range(NS)])
    y_syn = np.concatenate([short_hi, short_lo, short_hi, short_lo], 1)[order]
    z_syn = block_tiles(short_hi.T, short_lo.T)
    stacked = np.concatenate([hi, lo, hi, lo], 1)
    x_syn = np.full((SHARDS, 2, 12, 2, 128), zero)
    for half in range(2):
        x_syn[:, half, :, half] = stacked.reshape(SHARDS, 12, 128)
    x_syn = x_syn.reshape(192, 256)
    parts = []
    for t in (hi, lo):
        part = np.full((2, KEEP, SHARDS, 2, 12), zero)
        for half in range(2):
            part[half, :, :, half, :] = t.T.reshape(KEEP, SHARDS, 12)
        parts.append(part.reshape(64, 192))
    x_ana = np.concatenate(parts, 0)
    z_ana = np.concatenate([four_blocks(short_hi), four_blocks(short_lo)], 1)
    y_ana = np.concatenate([np.concatenate([t[order].T] * 2, 1) for t in (short_hi, short_lo)], 0)
    z_fit = block_tiles(fit_hi.T, fit_lo.T)
    rows = np.array([2 * (r % 32) + r // 32 for r in range(NS)])
    columns = np.array([4 * (r % 24) + r // 24 for r in range(NG)])
    y_fit = np.concatenate([t[rows][:, columns] for t in (fit_hi, fit_lo, fit_hi, fit_lo)], 1)
    return y_syn, z_syn, x_syn, x_ana, z_ana, y_ana, z_fit, y_fit


def kinetic_plane():
    def square(k):
        signed = jnp.where(k < KEEP // 2, k, k - KEEP)
        return (signed * signed).astype(F32) * (1.0 / (KEEP // 2) ** 2)

    ky = lax.broadcasted_iota(jnp.int32, (KEEP, KEEP * KEEP), 0)
    lane = lax.broadcasted_iota(jnp.int32, (KEEP, KEEP * KEEP), 1)
    return edge_energy * (square(ky) + square(lane // KEEP) + square(lane % KEEP))


def split(x):
    hi = x.astype(BF16)
    return hi, (x - hi.astype(F32)).astype(BF16)


def dot(a, b):
    return jnp.dot(a, b, preferred_element_type=F32)


def swap_groups(parts):
    lane = lax.broadcasted_iota(jnp.int32, parts[0].shape, 1)
    low = lane < 64
    even = lane % 64 < 32
    half = [None] * 4
    for j in range(2):
        half[j] = jnp.where(low, parts[j], pltpu.roll(parts[j + 2], 64, 1))
        half[j + 2] = jnp.where(low, pltpu.roll(parts[j], 64, 1), parts[j + 2])
    out = []
    for a, b in ((half[0], half[1]), (half[2], half[3])):
        out.append(jnp.where(even, a, pltpu.roll(b, 32, 1)))
        out.append(jnp.where(even, pltpu.roll(a, 96, 1), b))
    return out


def twofold(a, table, width):
    ah, al = split(a)
    wide = dot(ah, table[...])
    return wide[:, :width] + wide[:, width:] + dot(al, table[:, :width])


def spread_blocks(tiles, table):
    size = tiles.shape[0]
    table[...] = jnp.zeros(table.shape, BF16)
    for j in range(4):
        for part in range(2):
            column = 256 * part + 128 * (j // 2)
            source = 128 * (2 * part + j % 2)
            table[size * j : size * j + size, column : column + 128] = tiles[:, source : source + 128]


def fit_potential(v_ref, tabs, planes, own):
    z_fit, y_fit = tabs[6:]
    lane = lax.broadcasted_iota(jnp.int32, (32, 128), 1)
    low = lane < 64
    blank = jnp.zeros((4, 384), F32)
    blocks = []
    for c in range(24):
        blocks += [v_ref[:, 384 * c : 384 * c + 384], blank]
    fit = twofold(jnp.concatenate(blocks, 0), z_fit, 256)
    for tile in range(2):
        planes[tile] = fit[:, 128 * tile : 128 * tile + 128]
    columns = []
    for n in range(0, 12, 2):
        parts = []
        for j in range(4):
            a = planes[j // 2, pl.ds(n, 24, stride=16), :]
            b = planes[j // 2, pl.ds(n + 1, 24, stride=16), :]
            if j % 2 == 0:
                parts.append(jnp.where(low[:24], a, pltpu.roll(b, 64, 1)))
            else:
                parts.append(jnp.where(low[:24], pltpu.roll(a, 64, 1), b))
        columns.append(jnp.concatenate(parts, 0))
    hi, lo = split(jnp.concatenate(columns, 1))
    fit = dot(y_fit[...], jnp.concatenate([hi, hi, lo, lo], 0))
    for n in range(0, 12, 2):
        even, odd = fit[:32, 64 * n : 64 * n + 128], fit[32:, 64 * n : 64 * n + 128]
        first = jnp.where(low, even, pltpu.roll(odd, 64, 1))
        second = jnp.where(low, pltpu.roll(even, 64, 1), odd)
        for p, plane in ((n, first), (n + 1, second)):
            for half in range(2):
                for column in range(2):
                    t = 16 * half + 8 * column
                    own[pl.ds(192 * column + 12 * half + p, 8, stride=24), :] = plane[t : t + 8]


def expand_rows(c, tabs, scratch):
    y_syn, z_syn = tabs[:2]
    d1, d2h, d2l, _ = scratch
    ch, cl = split(c)
    along_y = dot(y_syn[...], jnp.concatenate([ch, ch, cl, cl], 0))
    for k8 in range(8):
        cols = slice(128 * k8, 128 * k8 + 128)
        parts = swap_groups([along_y[16 * j : 16 * j + 16, cols] for j in range(4)])
        for m in range(4):
            d1[pl.ds((4 * k8 + m) * 16, 16), :] = parts[m]
    for i in range(2):
        rows = jnp.concatenate([d1[pl.ds(8 * i + j, 32, stride=16), :] for j in range(8)], 0)
        dh, dl = split(twofold(rows, z_syn, 256))
        d2h[pl.ds(256 * i, 256), :] = dh
        d2l[pl.ds(256 * i, 256), :] = dl


def cross_planes(column, v, tabs, scratch):
    _, _, x_syn, x_ana = tabs[:4]
    _, d2h, d2l, bz = scratch

    def plane_step(i, carry):
        q = column * 4 + i
        r0 = pl.multiple_of(q * 32, 32)
        r1 = pl.multiple_of(q * 32 + 256, 32)
        h0, l0 = d2h[pl.ds(r0, 32), :], d2l[pl.ds(r0, 32), :]
        h1, l1 = d2h[pl.ds(r1, 32), :], d2l[pl.ds(r1, 32), :]
        field = dot(x_syn[...], jnp.concatenate([h0, h0, l0, l0, h1, h1, l1, l1], 0))
        tiles = [
            v[column, :, pl.ds(pl.multiple_of(48 * i + 24 * j, 8), 24), :].reshape(192, 128)
            for j in range(2)
        ]
        wh, wl = split(field * jnp.concatenate(tiles, 1))
        first = dot(x_ana[...], wh)
        back = first[:64] + first[64:] + dot(x_ana[pl.ds(0, 64), :], wl)
        bz[pl.ds(r0, 32), :] = back[:32]
        bz[pl.ds(r1, 32), :] = back[32:]
        return carry

    lax.fori_loop(0, 4, plane_step, 0, unroll=True)


def contract_rows(tabs, scratch):
    z_ana, y_ana = tabs[4:6]
    d1, _, _, bz = scratch
    for i in range(2):
        d1[pl.ds(256 * i, 256), :] = twofold(bz[pl.ds(256 * i, 256), :], z_ana, 128)
    columns = []
    for k8 in range(8):
        parts = [d1[pl.ds(4 * k8 + m, 16, stride=32), :] for m in range(4)]
        columns.append(jnp.concatenate(swap_groups(parts), 0))
    gh, gl = split(jnp.concatenate(columns, 1))
    back = dot(y_ana[...], jnp.concatenate([gh, gl], 0))
    return back[:32] + back[32:]


H_SCRATCH = [
    pltpu.VMEM((512, 128), F32),
    pltpu.VMEM((512, 256), BF16),
    pltpu.VMEM((512, 256), BF16),
    pltpu.VMEM((512, 256), F32),
]


def filter_kernel(x_hbm, v_hbm, rotation_hbm, lower, upper, owners, *refs):
    tables_hbm = refs[:8]
    filtered, residents = refs[8:10]
    x_ref, v_ref = refs[10:12]
    tabs = refs[12:20]
    scratch = refs[20:24]
    (v, planes, own, pack, coeffs, spread, landed, pairs, mate, gathered, blocks, relay, rotation_ref, left, rotated, local_sem,
     fit_tiles, syn_tiles, a_send, a_recv, v_send, v_recv, b_send, b_recv, c_send, c_recv, news) = refs[24:]
    band = lax.axis_index("band")
    grid = lax.axis_index("grid")
    z_hi, y, core, chip = band // 8, (band // 2) % 4, band % 2, band // 2
    z_lo, x = grid // 4, grid % 4
    sibling = (z_hi * 8 + y * 2 + 1 - core, grid)

    def z_step(step, other=0):
        z = (z_hi * 2 + z_lo + step) % 8
        return ((z // 2) * 8 + y * 2 + (core + other) % 2, (1 - z_lo) * 4 + x)

    def x_step(step):
        return (band, z_lo * 4 + (x + step) % 4)

    def y_step(step):
        return (z_hi * 8 + ((y + step) % 4) * 2 + core, grid)

    def remote(src, dst, send, recv, to):
        return pltpu.make_async_remote_copy(
            src_ref=src, dst_ref=dst, send_sem=send, recv_sem=recv, device_id=to, device_id_type=MESH
        )

    sources = (v_hbm, tables_hbm[6], tables_hbm[7], x_hbm, rotation_hbm) + tuple(tables_hbm[:6])
    targets = (v_ref, fit_tiles, tabs[7], x_ref, rotation_ref, tabs[0], syn_tiles) + tuple(tabs[2:6])
    fetches = [
        pltpu.make_async_copy(src, dst, local_sem.at[i])
        for i, (src, dst) in enumerate(zip(sources, targets))
    ]
    for fetch in fetches[:3]:
        fetch.start()

    barrier = pltpu.get_barrier_semaphore()
    neighbours = [z_step(step, other) for step in (1, 7) for other in range(2)]
    neighbours += [x_step(1), x_step(3), y_step(1), y_step(3), sibling]
    for to in neighbours:
        pl.semaphore_signal(barrier, inc=1, device_id=to, device_id_type=MESH)
    for fetch in fetches[3:]:
        fetch.start()

    def tell(turn):
        for to in (y_step(1), y_step(3)) if turn == 0 else (z_step(1), z_step(7)):
            pl.semaphore_signal(news.at[turn], inc=1, device_id=to, device_id_type=MESH)

    def hear(turn):
        pl.semaphore_wait(news.at[turn], 2)

    fetches[1].wait()
    spread_blocks(fit_tiles, tabs[6])
    fetches[0].wait()
    fetches[2].wait()
    fit_potential(v_ref, tabs, planes, own)
    for column in range(2):
        v[column, grid] = own[192 * column : 192 * column + 192]
    pl.semaphore_wait(barrier, len(neighbours))
    tell(0)

    def rows_of(ref, block, size):
        return ref.at[pl.ds(pl.multiple_of(block * size, size), size), :]

    def bring(to, block, slot):
        return remote(
            rows_of(pack, block, 32), rows_of(coeffs, slot, 32), a_send.at[0], a_recv.at[0], (band, to)
        )

    def all_rows(ref, sem):
        count = pl.ds(0, 224 if sem == 0 else 240)
        return remote(ref.at[count, :], ref.at[count, :], a_send.at[sem], a_recv.at[sem], sibling)

    near = [z_lo * 4 + (x + s) % 4 for s in (0, 3, 1, 2)]
    far = [(1 - z_lo) * 4 + (x + s) % 4 for s in (0, 3, 1, 2)]

    def v_copy(sem, shard, to, part=None, column=core):
        rows = pl.ds(0, 192) if part is None else pl.ds(96 * part, 96)
        ref = v.at[column, shard, rows, :]
        return remote(ref, ref, v_send.at[sem], v_recv.at[sem], to)

    sent = []

    def v_go(*where):
        copy = v_copy(*where)
        copy.start()
        sent.append(copy)

    def along_z(s, part):
        v_go(6 + 2 * s + part, near[s], z_step(7 if part else 1), part)

    def from_x(sem, s, part):
        v_copy(sem, near[s], sibling, part).wait_recv()
        along_z(s, part)

    def last_along_z(part):
        v_copy(4 + part, near[3], sibling, part).wait_recv()
        along_z(3, part)
        v_go(20 + part, near[3], z_step(7 if part else 1, 1), part)

    def from_z(s):
        for part in range(2):
            v_copy(6 + 2 * s + part, far[s], sibling, part).wait_recv()
        v_go(17 + s, far[s], sibling)

    v_go(0, near[0], x_step(1), 0)
    v_go(3, near[0], x_step(3), 1)
    v_go(1, near[0], x_step(1), 1)
    v_go(2, near[0], x_step(3), 0)
    along_z(0, 0)
    along_z(0, 1)
    fetches[3].wait()
    for r in range(32):
        pack[pl.ds(r, 8, stride=32), :] = x_ref[:, 128 * r : 128 * r + 128]
    partner = (1 - z_lo) * 4 + x
    by_z = remote(
        rows_of(pack, (1 - z_lo) * 4 + (x + 2) % 4, 32), relay, a_send.at[2], a_recv.at[2], (band, partner)
    )
    by_z.start()
    center = (lower[0] + upper[0]) * 0.5
    inverse = 1.0 / ((upper[0] - lower[0]) * 0.5)
    for fetch in fetches[4:]:
        fetch.wait()
    spread_blocks(syn_tiles, tabs[1])
    rh, rl = split(rotation_ref[...].T)
    left[...] = jnp.concatenate([rh, rl, rh, rl], 1)
    from_x(0, 1, 0)
    v_go(4, near[1], x_step(1), 0)
    from_x(3, 2, 1)
    v_go(5, near[2], x_step(3), 1)
    hear(0)
    tell(1)
    for dz, dx in ((0, 2), (1, 1), (1, 3), (1, 0), (0, 1), (0, 3)):
        to = (z_lo + dz) % 2 * 4 + (x + dx) % 4
        bring(to, to, grid).start()
    rows_of(coeffs, grid, 32)[...] = rows_of(pack, grid, 32)[...]
    by_z.wait_recv()
    remote(
        relay, rows_of(coeffs, partner, 32), a_send.at[0], a_recv.at[0], (band, z_lo * 4 + (x + 2) % 4)
    ).start()
    from_x(1, 1, 1)
    v_go(14, near[1], sibling)
    from_x(2, 2, 0)
    v_go(15, near[2], sibling)
    from_z(0)
    hear(1)
    last_along_z(0)
    last_along_z(1)
    v_go(16, near[3], sibling)
    tell(2)
    from_z(1)
    from_z(2)
    all_rows(coeffs, 0).wait_recv()
    c = jnp.concatenate([coeffs[pl.ds(k8, 32, stride=8), :] for k8 in range(8)], 1)
    expand_rows(c, tabs, scratch)
    for part in range(2):
        v_copy(12 + part, far[3], sibling, part).wait_recv()
    hear(2)
    tell(3)
    cross_planes(core, v, tabs, scratch)
    for s in range(1, 4):
        v_copy(13 + s, near[s], sibling, None, 1 - core).wait_recv()
    for s in range(3):
        v_copy(17 + s, far[s], sibling, None, 1 - core).wait_recv()
    for part in range(2):
        v_copy(20 + part, far[3], sibling, part, 1 - core).wait_recv()
    cross_planes(1 - core, v, tabs, scratch)
    shift = kinetic_plane() - center
    first = (shift * c + contract_rows(tabs, scratch)) * inverse
    hear(3)
    tell(4)
    expand_rows(first, tabs, scratch)
    cross_planes(0, v, tabs, scratch)
    cross_planes(1, v, tabs, scratch)
    second = shift * first + contract_rows(tabs, scratch)
    out = (2.0 * inverse) * second - c
    all_rows(coeffs, 0).wait_send()
    by_z.wait_send()
    for k8 in range(8):
        pack[pl.ds(k8, 32, stride=8), :] = out[:, 128 * k8 : 128 * k8 + 128]
    for k in range(2):
        spread[pl.ds(128 * k, 128), :] = pack[pl.ds(k, 128, stride=2), :]

    def bring_back(to, other):
        k = 1 - core if other else core
        return remote(
            rows_of(spread, k * 8 + to, 16), rows_of(landed, core * 8 + grid, 16),
            a_send.at[1], a_recv.at[1], (chip * 2 + k, to),
        )

    for d in range(1, SHARDS):
        for other in range(2):
            bring_back((grid + d) % SHARDS, other).start()
    bring_back(grid, 1).start()
    rows_of(landed, core * 8 + grid, 16)[...] = rows_of(spread, core * 8 + grid, 16)[...]
    for copy in sent:
        copy.wait_send()
    all_rows(landed, 1).wait_recv()
    for k in range(2):
        for i in range(CHIPS):
            pairs[i, k] = landed[pl.ds(128 * k + i, 8, stride=16), :]

    hear(4)

    for dz, dy in sorted(
        ((dz, dy) for dz in range(4) for dy in range(4) if dz + dy),
        key=lambda d: -2 * min(d[0], 4 - d[0]) - min(d[1], 4 - d[1]),
    ):
        to = (z_hi + dz) % 4 * 4 + (y + dy) % 4
        remote(pairs.at[to], blocks.at[chip], b_send.at[1], b_recv.at[1], (to * 2 + core, grid)).start()

    blocks[chip] = pairs[chip]
    swap = remote(pairs.at[:, 1 - core], mate, b_send.at[0], b_recv.at[0], sibling)
    swap.start()
    all_chips = remote(
        pairs.at[pl.ds(0, CHIPS - 1)], blocks.at[pl.ds(0, CHIPS - 1)], b_send.at[1], b_recv.at[1], sibling
    )
    all_chips.wait_recv()
    for s in range(STEPS):
        gathered[band, pl.ds(8 * s, 8), :] = blocks[owners[s] // 2, owners[s] % 2]

    def c_copy(sem, index, to):
        ref = gathered.at[index]
        return remote(ref, ref, c_send, c_recv.at[sem], (to, grid))

    def index_of(dz, dy):
        return ((z_hi + 4 - dz) % 4) * 8 + ((y + 4 - dy) % 4) * 2 + core

    def deliver(dz, dy):
        c_copy(16 + 4 * dz + dy, index_of(dz, dy), sibling[0]).start()

    def along_z_hi(dz):
        c_copy(dz, band, ((z_hi + dz) % 4) * 8 + band % 8).start()

    def along_y(dz):
        mine = index_of(dz, 0)
        for dy in (1, 3) if dz in CORNERS else (2, 1, 3):
            c_copy(4 + 3 * dz + dy - 1, mine, z_hi * 8 + ((y + dy) % 4) * 2 + core).start()
        deliver(dz, 0)

    def from_y(dz):
        for dy in (1, 3, 2):
            c_copy(4 + 3 * dz + dy - 1, index_of(dz, dy), sibling[0]).wait_recv()
            if dz == 0 and dy == 2:
                for corner in CORNERS:
                    c_copy(
                        4 + 3 * corner + 1, index_of(0, 2), ((z_hi + corner) % 4) * 8 + band % 8
                    ).start()
            deliver(dz, dy)

    def rotate(dz):
        for dy in range(4):
            twin = index_of(dz, dy) + 1 - 2 * core
            c_copy(16 + 4 * dz + dy, twin, sibling[0]).wait_recv()
        level = (z_hi + 4 - dz) % 4
        return columns_of(level * 8, 8, 1 + dz)

    def rotate_pair(dz, dy):
        twin = index_of(dz, dy) + 1 - 2 * core
        c_copy(16 + 4 * dz + dy, twin, sibling[0]).wait_recv()
        return columns_of(twin // 2 * 2, 2, 3 if dy == 0 else 4 + dy)

    def columns_of(first, count, sem):
        ah, al = split(jnp.concatenate([gathered[first + i] for i in range(count)], 1))
        at = pl.ds(pl.multiple_of(first * 128, 256), 128 * count)
        rotated[:, at] = dot(left[...], jnp.concatenate([ah, ah, al, al], 0))
        write = pltpu.make_async_copy(rotated.at[:, at], residents.at[:, at], local_sem.at[sem])
        write.start()
        writes.append(write)

    along_z_hi(1)
    along_z_hi(3)
    along_y(0)
    along_z_hi(2)
    for dz in (1, 3):
        c_copy(dz, index_of(dz, 0), sibling[0]).wait_recv()
        along_y(dz)
    swap.wait_recv()
    for i in range(CHIPS):
        x_ref[:, pl.ds(pl.multiple_of(256 * i + 128 * core, 128), 128)] = pairs[i, core]
        x_ref[:, pl.ds(pl.multiple_of(256 * i + 128 - 128 * core, 128), 128)] = mate[i]
    write = pltpu.make_async_copy(x_ref, filtered, local_sem.at[0])
    write.start()
    from_y(0)
    c_copy(2, index_of(2, 0), sibling[0]).wait_recv()
    along_y(2)
    writes = [write]
    rotate(0)
    from_y(1)
    from_y(3)
    rotate(1)
    from_y(2)
    rotate(3)
    for dy in (0, 1, 3, 2):
        rotate_pair(2, dy)
    all_chips.wait_send()
    all_rows(landed, 1).wait_send()
    swap.wait_send()
    every = pl.ds(0, GROUPS - 1)
    remote(gathered.at[every], gathered.at[every], c_send, c_recv.at[0], sibling).wait_send()
    for copy in writes:
        copy.wait()


SMEM = pl.BlockSpec(memory_space=pltpu.SMEM)
ANY = pl.BlockSpec(memory_space=pl.ANY)
FILTER = pl.pallas_call(
    filter_kernel,
    out_shape=(
        jax.ShapeDtypeStruct((8, 4096), F32),
        jax.ShapeDtypeStruct((192, 4096), F32),
    ),
    in_specs=[ANY] * 3 + [SMEM] * 3 + [ANY] * 8,
    out_specs=(ANY, ANY),
    scratch_shapes=[
        pltpu.VMEM((8, 4096), F32),
        pltpu.VMEM((12, 9216), F32),
        pltpu.VMEM((64, 128), BF16),
        pltpu.VMEM((128, 512), BF16),
        pltpu.VMEM((192, 256), BF16),
        pltpu.VMEM((128, 192), BF16),
        pltpu.VMEM((256, 256), BF16),
        pltpu.VMEM((64, 128), BF16),
        pltpu.VMEM((384, 512), BF16),
        pltpu.VMEM((64, 384), BF16),
    ] + H_SCRATCH + [
        pltpu.VMEM((2, SHARDS, 192, 128), F32),
        pltpu.VMEM((2, 384, 128), F32),
        pltpu.VMEM((384, 128), F32),
        pltpu.VMEM((256, 128), F32),
        pltpu.VMEM((256, 128), F32),
        pltpu.VMEM((256, 128), F32),
        pltpu.VMEM((256, 128), F32),
        pltpu.VMEM((CHIPS, 2, 8, 128), F32),
        pltpu.VMEM((CHIPS, 8, 128), F32),
        pltpu.VMEM((GROUPS, 64, 128), F32),
        pltpu.VMEM((CHIPS, 2, 8, 128), F32),
        pltpu.VMEM((32, 128), F32),
        pltpu.VMEM((64, 192), F32),
        pltpu.VMEM((192, 256), BF16),
        pltpu.VMEM((192, 4096), F32),
        pltpu.SemaphoreType.DMA((11,)),
        pltpu.VMEM((96, 512), BF16),
        pltpu.VMEM((32, 512), BF16),
        pltpu.SemaphoreType.DMA((3,)),
        pltpu.SemaphoreType.DMA((3,)),
        pltpu.SemaphoreType.DMA((22,)),
        pltpu.SemaphoreType.DMA((22,)),
        pltpu.SemaphoreType.DMA((2,)),
        pltpu.SemaphoreType.DMA((2,)),
        pltpu.SemaphoreType.DMA,
        pltpu.SemaphoreType.DMA((32,)),
        pltpu.SemaphoreType.REGULAR((5,)),
    ],
    compiler_params=pltpu.CompilerParams(
        collective_id=0, has_side_effects=True, vmem_limit_bytes=VMEM_LIMIT
    ),
    name="filter",
)


def write_kernel(filtered, residents, filtered_out, residents_out, block, rows, in_sem, out_sem):
    parts = [(filtered, block, filtered_out)]
    for i in range(8):
        at = pl.ds(24 * i, 24)
        parts.append((residents.at[at, :], rows.at[at, :], residents_out.at[at, :]))
    reads = [pltpu.make_async_copy(a, b, in_sem.at[i]) for i, (a, b, _) in enumerate(parts)]
    writes = [pltpu.make_async_copy(b, c, out_sem.at[i]) for i, (_, b, c) in enumerate(parts)]
    for read in reads:
        read.start()
    for read, write in zip(reads, writes):
        read.wait()
        write.start()
    for write in writes:
        write.wait()


WRITE = pl.pallas_call(
    write_kernel,
    out_shape=(
        jax.ShapeDtypeStruct((8, 4096), F32),
        jax.ShapeDtypeStruct((192, 4096), F32),
    ),
    in_specs=[ANY] * 2,
    out_specs=(ANY, ANY),
    scratch_shapes=[
        pltpu.VMEM((8, 4096), F32),
        pltpu.VMEM((192, 4096), F32),
        pltpu.SemaphoreType.DMA((9,)),
        pltpu.SemaphoreType.DMA((9,)),
    ],
    compiler_params=pltpu.CompilerParams(vmem_limit_bytes=VMEM_LIMIT),
    name="write",
)


def body(block_coeffs, potential, lower_edge, upper_edge, rotation, owners):
    consts = [jnp.asarray(t) for t in tables()]
    coefficients = rotation.transpose(0, 2, 1).reshape(64, 192)
    return tuple(
        WRITE(*FILTER(block_coeffs, potential, coefficients, lower_edge, upper_edge, owners, *consts))
    )


def solution(mesh):
    return jax.shard_map(
        body,
        mesh=mesh,
        in_specs=(P("band", "grid"), P("grid", None), P(), P(), P(None, "band", None), P()),
        out_specs=(P("band", "grid"), P("band", "grid")),
        check_vma=False,
    )
```
